512 devices in a mesh: slab: 64 (over x, z, core), dp: 8 (over y).
Axes of the slice: x: 4, y: 8, z: 8, core: 2. Of those that a mesh axis runs over, the one named last changes fastest.
Arguments:
- point_feats: float32 [8, 32768, 128], P('dp', 'slab'), may hold values from -6 to 6
- owner_slab: int32 [8, 32768, 1], P('dp', 'slab'), may hold values from 0 to 63; in each aligned block of 512 rows (0 to 511, 512 to 1023, ..., all dimensions but the last counted through in order) at most 16 rows name the same one
- block_slot: int32 [8, 32768], P('dp', 'slab'), may hold values from 0 to 1
- voxel_index: int32 [8, 32768], P('dp', 'slab'), may hold values from 0 to 511
- boundary: int32 [8, 64, 2, 1], P('dp', 'slab'), may hold values from 0 to 1, as said below
- neighbours: int32 [8, 128, 27], P('dp', 'slab'), may hold values from 0 to 4, as said below
- weight_taps: float32 [27, 128, 128], replicated, may hold values from -0.109375 to 0.109375
- cotangent: float32 [8, 65536, 128], P('dp', 'slab'), may hold values from -6 to 6
Outputs:
- activated: float32 [8, 65536, 128], P('dp', 'slab')
- point_grads: float32 [8, 32768, 128], P('dp', 'slab')
- weight_grads: float32 [3456, 128], P('slab')
The draws below stay inside these ranges and needn't reach their ends.
Inputs may be any that keep to these rules, and one draw needn't show every extreme that they name: `owner_slab`: among the points of one device, no slab is named by more than 16 points, and exactly 16 in some device. `boundary`: each list of one slab holds 1 different block slots. `neighbours`: entry 13 of a block's row is the block's own slot. Entries 0 to 8 name a block of the slab (below 2), one of the 1 block from the slab before (2 to 2), or the zero block 4; entries 18 to 26 a block of the slab, one of the 1 block from the slab after, or the zero block; the others a block of the slab or the zero block.
All inputs are finite; a program needn't handle non-finite values.
Results may differ from the reference program's by a relative error of at most 0.0003.
Values sent between devices are 32-bit elements; how exact they have to be, the bound alone decides.
A program may use at most 64 MiB of HBM per device.

```python
import math
import jax
import jax.numpy as jnp
import numpy as np
from jax import lax

C = 128
E = 8
NB = 2
NH = 1
P_DEV = 512
VOX = 512
CAP = 16
WIN = 8
N_SLAB = 64


def draw_boundary(key, part):
    subkeys = jax.random.split(jax.random.fold_in(key, 11), WIN * N_SLAB * 2)
    chosen = jax.vmap(lambda subkey: jax.random.permutation(subkey, NB)[:NH])(subkeys)
    return chosen.reshape(WIN, N_SLAB, 2, NH).astype(jnp.int32)


def draw_neighbours(key, part):
    raw_values = jax.random.randint(jax.random.fold_in(key, 7), (WIN, N_SLAB * NB, 27), 0, NB + NH + 1)
    column = jnp.arange(27)[None, None, :]
    offset_x = column // 9
    empty_slot = NB + 2 * NH
    lower = jnp.where(raw_values < NB + NH, raw_values, empty_slot)
    upper = jnp.where(raw_values < NB, raw_values, jnp.where(raw_values < NB + NH, raw_values + NH, empty_slot))
    middle = jnp.where(raw_values < NB, raw_values, empty_slot)
    chosen = jnp.where(offset_x == 0, lower, jnp.where(offset_x == 2, upper, middle))
    own_slot = (jnp.arange(N_SLAB * NB) % NB)[None, :, None]
    chosen = jnp.where(column == 13, own_slot, chosen)
    return chosen.astype(jnp.int32)


def touch_ends(entries, own_key, least, largest):
    longest = entries.shape.index(max(entries.shape))
    spots = []
    for shift in (0, 1):
        where = [jax.random.randint(jax.random.fold_in(own_key, axis), (), 0, length) for axis, length in enumerate(entries.shape)]
        where[longest] = (where[longest] + shift) % entries.shape[longest]
        spots.append(tuple(where))
    return entries.at[spots[0]].set(least).at[spots[1]].set(largest)


def steps_of(rng, dims, cuts, low, largest):
    loudness = 1.0
    for dim, shards_of in cuts:
        heights = jax.random.uniform(jax.random.fold_in(jax.random.fold_in(rng, 6), dim), (shards_of,), jnp.float32, low / len(cuts), largest / len(cuts))
        loudness = loudness * jnp.repeat(jnp.exp(heights), dims[dim] // shards_of).reshape((-1,) + (1,) * (len(dims) - 1 - dim))
    return loudness


def deal_out(stream_key, own, number, rows, amount, top, bound, skew):
    sequence = jax.random.permutation(stream_key, amount)
    packed, usual = shares(amount, rows * top, bound, skew, True), shares(amount, rows * top, bound, skew, False)
    places = jnp.arange(amount)

    def named(tallies, offset_by):
        used = int((tallies > 0).sum())
        fixed = max(1, used // 4)
        passed = fixed + (places - fixed + offset_by * (used - fixed)) % max(1, amount - fixed)
        return jnp.zeros((amount,), jnp.int32).at[sequence[jnp.where(places < fixed, places, passed)]].set(jnp.asarray(tallies, jnp.int32))

    tallies = jnp.where(number % 4 == 0, named(packed, number // 4), named(usual, number - number // 4 - 1))
    mixed = jax.random.permutation(jax.random.fold_in(own, 3), amount)
    source_of, receiver = mixed[0:amount // 2 * 2:2], mixed[1:amount // 2 * 2:2]
    margin = jnp.minimum(tallies[source_of] - 1, bound - tallies[receiver]) // 2
    margin = jnp.where((source_of == sequence[0]) | (receiver == sequence[0]) | (tallies[receiver] == 0), 0, jnp.maximum(margin, 0))
    passed = jax.random.randint(jax.random.fold_in(own, 4), (amount // 2,), 0, 1 << 20) % (margin + 1)
    tallies = tallies.at[source_of].add(-passed).at[receiver].add(passed)
    members = jnp.searchsorted(jnp.cumsum(tallies), jnp.arange(rows * top), side="right").astype(jnp.int32)
    table = members.reshape(top, rows).T
    table = table[jax.random.permutation(jax.random.fold_in(own, 1), rows)]
    offset_by = jax.random.randint(jax.random.fold_in(own, 2), (rows, 1), 0, top)
    return jnp.take_along_axis(table, (jnp.arange(top)[None, :] + offset_by) % top, axis=1)


def shares(count, total, bound, lean, full):
    weights = [(1 << 20) // math.isqrt(standing ** lean) + 1 for standing in range(1, count + 1)]
    largest = bound if full else min(bound, max(-(-total // count), total * weights[0] // sum(weights)))
    least = 1 if total - largest >= count - 1 else 0
    given, surplus = [largest] + [least] * (count - 1), total - largest - least * (count - 1)
    while surplus > 0:
        movable = [i for i in range(1, count) if given[i] < largest] or [i for i in range(1, count) if given[i] < bound]
        pool, left = sum([weights[i] for i in movable]), surplus
        for i in movable:
            addition = min(bound - given[i], max(1, left * weights[i] // pool), surplus)
            given[i] = given[i] + addition
            surplus = surplus - addition
    return np.array(given)


def centred(stream_key, extent, spread, most, cuts=(), held_as=jnp.bfloat16):
    drawn = jax.random.normal(stream_key, extent, jnp.float32) * spread
    if len(cuts) > 0:
        drawn = steps_of(stream_key, extent, cuts, -0.22, 0.18) * drawn
    return jnp.clip(drawn, min=-most, max=most).astype(held_as)


def setup_inputs(seed: int = 0) -> dict:
    key_of = jax.random.split(jax.random.key(seed), 9)
    point_feats = centred(key_of[0], (WIN, N_SLAB * P_DEV, C), 1.0, 6.0, ((0, 8), (1, 64)), jnp.float32)
    owner_slab_keys = jax.random.split(jax.random.fold_in(key_of[1], 1), WIN * (N_SLAB * P_DEV) // P_DEV)
    owner_slab_turns = jax.random.permutation(jax.random.fold_in(key_of[1], 3), WIN * (N_SLAB * P_DEV) // P_DEV)
    owner_slab = jax.vmap(lambda own, number: deal_out(jax.random.fold_in(key_of[1], 2), own, number, P_DEV, N_SLAB, 1, CAP, 2))(owner_slab_keys, owner_slab_turns).reshape((WIN, N_SLAB * P_DEV, 1))
    block_slot = touch_ends(jax.random.randint(key_of[2], (WIN, N_SLAB * P_DEV), 0, NB), jax.random.fold_in(key_of[2], 1), 0, NB - 1).astype(jnp.int32)
    voxel_index = touch_ends(jax.random.randint(key_of[3], (WIN, N_SLAB * P_DEV), 0, VOX), jax.random.fold_in(key_of[3], 1), 0, VOX - 1).astype(jnp.int32)
    boundary = draw_boundary(jax.random.fold_in(key_of[8], 71), 0)
    neighbours = draw_neighbours(jax.random.fold_in(key_of[8], 71), 0)
    weight_taps = centred(key_of[6], (27, C, C), (27 * C) ** -0.5, 0.109375, (), jnp.float32)
    cotangent = centred(key_of[7], (WIN, N_SLAB * NB * VOX, C), 1.0, 6.0, ((0, 8), (1, 64)), jnp.float32)
    return dict(point_feats=point_feats, owner_slab=owner_slab, block_slot=block_slot, voxel_index=voxel_index, boundary=boundary, neighbours=neighbours, weight_taps=weight_taps, cotangent=cotangent)


highest = lax.Precision.HIGHEST

def grid_tables():
    padded_edge = E + 2
    position = np.arange(padded_edge)
    section = np.where(position == 0, 0, np.where(position == padded_edge - 1, 2, 1))
    within = np.where(position == 0, E - 1, np.where(position == padded_edge - 1, 0, position - 1))
    grid_x, grid_y, grid_z = np.meshgrid(position, position, position, indexing='ij')
    tap_table = section[grid_x] * 9 + section[grid_y] * 3 + section[grid_z]
    voxel_table = within[grid_x] * E * E + within[grid_y] * E + within[grid_z]
    return (jnp.asarray(tap_table.reshape(-1), jnp.int32), jnp.asarray(voxel_table.reshape(-1), jnp.int32))

def slab_work(visible, neighbour_rows, weight_taps, grad_out):
    tap_table, voxel_table = grid_tables()
    slots_all = visible.shape[0]
    flat_visible = visible.reshape(slots_all * VOX, C)
    gather_rows = (neighbour_rows[:, tap_table] * VOX + voxel_table[None, :]).astype(jnp.int32)
    padded = flat_visible[gather_rows].reshape(NB, E + 2, E + 2, E + 2, C)
    pre_act = jnp.zeros((NB * VOX, C), jnp.float32)
    for tap_x in range(3):
        for tap_y in range(3):
            for tap_z in range(3):
                window = padded[:, tap_x:tap_x + E, tap_y:tap_y + E, tap_z:tap_z + E].reshape(NB * VOX, C)
                pre_act = pre_act + jnp.dot(window, weight_taps[tap_x * 9 + tap_y * 3 + tap_z], precision=highest, preferred_element_type=jnp.float32)
    gate_value = jax.nn.sigmoid(pre_act)
    activated = pre_act * gate_value
    grad_pre = grad_out * gate_value * (1.0 + pre_act * (1.0 - gate_value))
    grad_padded = jnp.zeros_like(padded)
    pieces = []
    for tap_x in range(3):
        for tap_y in range(3):
            for tap_z in range(3):
                window = padded[:, tap_x:tap_x + E, tap_y:tap_y + E, tap_z:tap_z + E].reshape(NB * VOX, C)
                pieces.append(jnp.dot(window.T, grad_pre, precision=highest, preferred_element_type=jnp.float32))
                back_rows = jnp.dot(grad_pre, weight_taps[tap_x * 9 + tap_y * 3 + tap_z].T, precision=highest, preferred_element_type=jnp.float32)
                grad_padded = grad_padded.at[:, tap_x:tap_x + E, tap_y:tap_y + E, tap_z:tap_z + E].add(back_rows.reshape(NB, E, E, E, C))
    weight_term = jnp.stack(pieces).reshape(27 * C, C)
    grad_visible = jnp.zeros((slots_all * VOX, C), jnp.float32).at[gather_rows.reshape(-1)].add(grad_padded.reshape(-1, C))
    return (activated, grad_visible.reshape(slots_all, VOX, C), weight_term)

def reference(point_feats, owner_slab, block_slot, voxel_index, boundary, neighbours, weight_taps, cotangent):
    row_ids = ((owner_slab[:, :, 0] * NB + block_slot) * VOX + voxel_index).astype(jnp.int32)

    def voxelize(rows_one, feats_one):
        return jnp.zeros((N_SLAB * NB * VOX, C), jnp.float32).at[rows_one].add(feats_one)
    block_feats = jax.vmap(voxelize)(row_ids, point_feats).reshape(WIN, N_SLAB, NB, VOX, C)
    before = jnp.roll(block_feats, 1, axis=1)
    after_slab = jnp.roll(block_feats, -1, axis=1)
    bound_before = jnp.roll(boundary, 1, axis=1)[:, :, 1]
    bound_after = jnp.roll(boundary, -1, axis=1)[:, :, 0]
    pick_rows = jax.vmap(jax.vmap(lambda blocks, chosen: blocks[chosen]))
    from_left = pick_rows(before, bound_before)
    from_right = pick_rows(after_slab, bound_after)
    empty_block = jnp.zeros((WIN, N_SLAB, 1, VOX, C), jnp.float32)
    visible = jnp.concatenate([block_feats, from_left, from_right, empty_block], axis=2)
    slots_all = NB + 2 * NH + 1
    visible_items = visible.reshape(WIN * N_SLAB, slots_all, VOX, C)
    neighbour_items = neighbours.reshape(WIN * N_SLAB, NB, 27)
    cotangent_items = cotangent.reshape(WIN * N_SLAB, NB * VOX, C)

    def scan_step(running, item_tuple):
        activated, grad_visible, weight_term = slab_work(item_tuple[0], item_tuple[1], weight_taps, item_tuple[2])
        return (running + weight_term, (activated, grad_visible))
    weight_sum, (activated, grad_visible) = lax.scan(scan_step, jnp.zeros((27 * C, C), jnp.float32), (visible_items, neighbour_items, cotangent_items))
    grad_visible = grad_visible.reshape(WIN, N_SLAB, slots_all, VOX, C)
    grad_own = grad_visible[:, :, :NB]
    left_grads = grad_visible[:, :, NB:NB + NH]
    right_grads = grad_visible[:, :, NB + NH:NB + 2 * NH]
    add_at = jax.vmap(jax.vmap(lambda blocks, chosen, additions: blocks.at[chosen].add(additions)))
    grad_blocks = add_at(grad_own, boundary[:, :, 0], jnp.roll(right_grads, 1, axis=1))
    grad_blocks = add_at(grad_blocks, boundary[:, :, 1], jnp.roll(left_grads, -1, axis=1))
    point_grads = jax.vmap(lambda flat_rows, row_list: flat_rows[row_list])(grad_blocks.reshape(WIN, N_SLAB * NB * VOX, C), row_ids)
    activated = activated.reshape(WIN, N_SLAB * NB * VOX, C)
    scale = 1.0 / math.sqrt(WIN * N_SLAB * NB * VOX)
    return (activated, point_grads, weight_sum * scale)
```

```python
import functools
import math

import jax
import jax.numpy as jnp
from jax import lax
from jax.experimental import pallas as pl
from jax.experimental.pallas import tpu as pltpu
from jax.sharding import PartitionSpec as P

C = 128
E = 8
NB = 2
PTS = 512
VOX = 512
ROWS = NB * VOX
TAPS = 27
SLOTS = 2 * PTS
f32 = jnp.float32
bf16 = jnp.bfloat16
i32 = jnp.int32
MESH = pl.DeviceIdType.MESH
highest = lax.Precision.HIGHEST
LIMIT = 60 * 1024 * 1024
PLACES = {64: (4, 8, 2), 8: (2, 2, 2), 4: (2, 1, 2)}


def iota(shape, dim):
    return lax.broadcasted_iota(i32, shape, dim)


def split(v):
    hi = v.astype(bf16)
    return hi, (v - hi.astype(f32)).astype(bf16)


def hilo(v):
    return jnp.concatenate(split(v), axis=-1)


def onehot(where):
    return jnp.where(where, 1.0, 0.0).astype(bf16)


def fold(v):
    return v[:, :C] + v[:, C:]


def dot(a, b):
    return lax.dot_general(a, b, (((1,), (0,)), ((), ())), preferred_element_type=f32)


def column(row):
    return jnp.transpose(jnp.broadcast_to(row, (8, row.shape[1])))[:, 0:1]


def pack_points(n, me, feats, own, vid, sbuf, place, idrows):
    cap = SLOTS // n
    group = C // cap
    ownr = own[...].astype(f32)
    ownc = column(ownr)
    first = iota((PTS, PTS), 0) < iota((PTS, PTS), 1)
    same = (ownc == ownr) & first
    rank = jnp.sum(jnp.where(same, 1.0, 0.0), axis=0, keepdims=True)
    placed = ownr * cap + rank
    place[...] = placed
    x2 = hilo(feats[...])
    pick = onehot(iota((SLOTS, PTS), 0).astype(f32) == placed)
    rows = fold(dot(pick, x2))
    sbuf[:, 0:cap, :] = rows.reshape(n, cap, C)
    lane = iota((PTS, C), 1).astype(f32)
    shift = (lax.rem(me, group) * cap).astype(f32)
    to_lane = jnp.where(lane == column(rank) + shift, 1.0, 0.0)
    ids = vid[...].astype(f32) + 1.0
    to_dest = jnp.where(iota((n, PTS), 0).astype(f32) == ownr, ids, 0.0)
    idrows[...] = lax.dot_general(
        to_dest, to_lane, (((1,), (0,)), ((), ())), precision=highest, preferred_element_type=f32
    )

    def put(d, carry):
        sbuf[d, cap : cap + 1, :] = idrows[pl.ds(d, 1), :]
        return carry

    lax.fori_loop(0, n, put, 0)


def prepare_taps(w, wp):
    def step(t, carry):
        rows = pl.ds(pl.multiple_of(t * 384, 384), 384)
        wp[rows, :] = hilo(w[rows, :])
        return carry

    lax.fori_loop(0, 9, step, 0)


def voxelize(n, rbuf, ids8, x2s, vis):
    cap = SLOTS // n
    group = C // cap
    x2s[...] = hilo(rbuf[:, 0:cap, :].reshape(SLOTS, C))
    ids = rbuf[:, cap : cap + 1, :].reshape(8, group, 1, C).sum(axis=1)
    ids8[...] = ids - 1.0

    def step(t, carry):
        vox = (iota((256, C), 0) + t * 256).astype(f32)
        pick = jnp.concatenate([onehot(vox == ids8[r]) for r in range(8)], axis=1)
        rows = pl.ds(pl.multiple_of(t * 256, 256), 256)
        vis[rows, :] = fold(dot(pick, x2s[...]))
        return carry

    lax.fori_loop(0, 4, step, 0)


SEC_P = ((slice(0, 1), slice(7, 8)), (slice(1, 9), slice(0, 8)), (slice(9, 10), slice(0, 1)))


def sections():
    for i in range(3):
        for j in range(3):
            if i == 1 and j == 1:
                for p in range(8):
                    yield i, j, slice(p + 1, p + 2), slice(1, 9), slice(p, p + 1), slice(0, 8)
            else:
                (ps, xs), (qs, ys) = SEC_P[i], SEC_P[j]
                yield i, j, ps, qs, xs, ys


def build_windows(nb, vis, S):
    for i, j, ps, qs, xs, ys in sections():
        e = 9 * i + 3 * j
        parts = ([], [], [])
        for b in range(NB):
            mid = vis[nb[b, e + 1], xs, ys]
            low = vis[nb[b, e], xs, ys]
            high = vis[nb[b, e + 2], xs, ys]
            z = iota(mid.shape, 2)
            parts[0].append(jnp.roll(jnp.where(z == 7, low, mid), 1, axis=2))
            parts[1].append(mid)
            parts[2].append(jnp.roll(jnp.where(z == 0, high, mid), -1, axis=2))
        for k in range(3):
            hi, lo = split(jnp.concatenate(parts[k], axis=2))
            S[ps, qs, :, k * C : (k + 1) * C] = hi
            S[ps, qs, :, (3 + k) * C : (4 + k) * C] = lo


def forward(S, wp, cot, act, G4, GT):
    def step(m, carry):
        total = None
        for part in range(2):
            wins = []
            for i in range(3):
                for j in range(3):
                    win = S[pl.ds(2 * m + i, 2), j : j + 8, :, part * 384 : part * 384 + 384]
                    wins.append(win.reshape(256, 384))
            got = dot(jnp.concatenate(wins, axis=1), wp[...])
            total = got if total is None else total + got
        pre = fold(total).reshape(2, 8, 16, C)
        gate = 1.0 / (1.0 + jnp.exp(-pre))
        xs = pl.ds(2 * m, 2)
        out = pre * gate
        for b in range(NB):
            act[b, xs] = out[:, :, 8 * b : 8 * b + 8]
        up = jnp.concatenate([cot[b, xs] for b in range(NB)], axis=2)
        g = (up * gate * (1.0 + pre * (1.0 - gate))).reshape(256, C)
        hi, lo = split(g)
        rows = pl.ds(pl.multiple_of(256 * m, 256), 256)
        G4[rows, :] = jnp.concatenate([hi, hi, lo, lo], axis=1)
        gt = jnp.transpose(g)
        thi, tlo = split(gt)
        GT[m, 0:C, :] = thi
        GT[m, C : 2 * C, :] = tlo
        return carry

    lax.fori_loop(0, 4, step, 0)


def weight_grad(S, GT, dW, scale):
    def step(ij, carry):
        i, j = ij // 3, lax.rem(ij, 3)
        total = None
        for m in range(4):
            win = S[pl.ds(i + 2 * m, 2), pl.ds(j, 8)].reshape(256, 768)
            got = dot(GT[m], win)
            total = got if total is None else total + got
        both = total[:C] + total[C:]
        for k in range(3):
            one = both[:, k * C : (k + 1) * C] + both[:, (3 + k) * C : (4 + k) * C]
            rows = pl.ds(pl.multiple_of(ij * 384 + k * C, C), C)
            dW[rows, :] = jnp.transpose(one) * scale
        return carry

    lax.fori_loop(0, 9, step, 0)


def input_grad(G4, wp, A):
    A[...] = jnp.zeros_like(A)

    def step(ij, carry):
        i, j = ij // 3, lax.rem(ij, 3)
        w = wp[pl.ds(pl.multiple_of(ij * 384, 384), 384), :]
        w2 = jnp.concatenate([w, w], axis=1)
        for m in range(4):
            y = lax.dot_general(
                G4[m * 256 : (m + 1) * 256, :], w2, (((1,), (1,)), ((), ())), preferred_element_type=f32
            )
            for k in range(3):
                A[k, pl.ds(i + 2 * m, 2), pl.ds(j, 8)] += y[:, k * C : (k + 1) * C].reshape(2, 8, 16, C)
        return carry

    lax.fori_loop(0, 9, step, 0)


def carry_back(nb, A, grad, lent):
    grad[...] = jnp.zeros_like(grad)
    lent[...] = jnp.zeros_like(lent)
    for i, j, ps, qs, xs, ys in sections():
        e = 9 * i + 3 * j
        for b in range(NB):
            a0, a1, a2 = (A[k, ps, qs, 8 * b : 8 * b + 8, :] for k in range(3))
            z = iota(a0.shape, 2)
            a0 = jnp.roll(a0, -1, axis=2)
            a2 = jnp.roll(a2, 1, axis=2)
            mid = a1 + jnp.where(z == 7, 0.0, a0) + jnp.where(z == 0, 0.0, a2)
            low = jnp.where(z == 7, a0, 0.0)
            high = jnp.where(z == 0, a2, 0.0)

            def share(t):
                part = jnp.where(nb[b, e] == t, low, 0.0) + jnp.where(nb[b, e + 2] == t, high, 0.0)
                if i == 1 and j == 1:
                    return part + mid if t == b else part
                return part + jnp.where(nb[b, e + 1] == t, mid, 0.0)

            for t in range(NB):
                grad[t, xs, ys] += share(t)
            if i == 0:
                lent[0, ys] += share(2)[0]
            if i == 2:
                lent[1, ys] += share(3)[0]


def chunk_rows(n):
    return TAPS * C // n


def padded_rows(n):
    return -(-chunk_rows(n) // 8) * 8


def cut_chunks(n, dW, dwc):
    X, Z, K = PLACES[n]
    size, pad = chunk_rows(n), padded_rows(n)
    for d in range(n):
        dwc[d % K, d // K // Z, d // K % Z] = dW[size * d : size * d + pad, :]


def greet(n, wins, me, y, columns):
    barrier = pltpu.get_barrier_semaphore()

    def hello(o, carry):
        pl.semaphore_signal(barrier, inc=1, device_id=(lax.rem(me + o, n), y), device_id_type=MESH)
        return carry

    lax.fori_loop(1, n, hello, 0)
    if columns:

        def hello_y(o, carry):
            pl.semaphore_signal(barrier, inc=1, device_id=(me, lax.rem(y + o, wins)), device_id_type=MESH)
            return carry

        lax.fori_loop(1, wins, hello_y, 0)


def greeted(n, wins, columns):
    pl.semaphore_wait(pltpu.get_barrier_semaphore(), n - 1 + (wins - 1 if columns else 0))


def spread(n, me, y, src, dst, ssem, rsem):
    def send(o, carry):
        d = lax.rem(me + o, n)
        pltpu.make_async_remote_copy(
            src_ref=src.at[d], dst_ref=dst.at[me], send_sem=ssem, recv_sem=rsem, device_id=(d, y), device_id_type=MESH
        ).start()
        return carry

    lax.fori_loop(1, n, send, 0)


def all_of(count, ref, sem):
    pltpu.make_async_copy(ref.at[pl.ds(0, count)], ref.at[pl.ds(0, count)], sem).wait()


def arrive(n, wins, feats, own, vid, bnd, w, vis, halo, ids8, place, wp, sbuf, rbuf, idrows, x2s, hs, hr, sems):
    me, y = lax.axis_index("slab"), lax.axis_index("dp")
    greet(n, wins, me, y, False)
    pack_points(n, me, feats, own, vid, sbuf, place, idrows)
    greeted(n, wins, False)
    spread(n, me, y, sbuf, rbuf, sems.at[0], sems.at[1])
    rbuf[me] = sbuf[me]
    prepare_taps(w, wp)
    all_of(n - 1, rbuf, sems.at[1])
    voxelize(n, rbuf, ids8, x2s, vis)
    hs[0] = jnp.where(bnd[1] == 1, vis[VOX + 448 : VOX + 512, :], vis[448:512, :])
    hs[1] = jnp.where(bnd[0] == 1, vis[VOX : VOX + 64, :], vis[0:64, :])
    copies = exchange(n, me, y, hs, hr, sems)
    all_of(n - 1, sbuf, sems.at[0])
    for copy in copies:
        copy.wait()
    halo[...] = hr[...]


def exchange(n, me, y, hs, hr, sems):
    copies = []
    for side, to in ((0, lax.rem(me + 1, n)), (1, lax.rem(me + n - 1, n))):
        copy = pltpu.make_async_remote_copy(
            src_ref=hs.at[side],
            dst_ref=hr.at[side],
            send_sem=sems.at[2 + side],
            recv_sem=sems.at[4 + side],
            device_id=(to, y),
            device_id_type=MESH,
        )
        copy.start()
        copies.append(copy)
    return copies


def middle(n, scale, own, halo, cot, wp, nb, act, dwc, grad, lent, vis, S, G4, GT, dW, A):
    vis[0:2] = own[...]
    vis[2, 7:8] = halo[0:1]
    vis[3, 0:1] = halo[1:2]
    vis[4] = jnp.zeros((8, 8, 8, C), f32)
    build_windows(nb, vis, S)
    forward(S, wp, cot, act, G4, GT)
    weight_grad(S, GT, dW, scale)
    cut_chunks(n, dW, dwc)
    input_grad(G4, wp, A)
    carry_back(nb, A, grad, lent)


def leave(n, wins, dwc, grad, lent, bnd, ids8, place, pts, total, core_r, xs_, x_r, zs_, z_r, ys_, y_r, hr, gfull, x2s, sbuf, rbuf, sems, rsems):
    X, Z, K = PLACES[n]
    cap = SLOTS // n
    me, y = lax.axis_index("slab"), lax.axis_index("dp")
    core = lax.rem(me, K)
    z = lax.rem(me // K, Z)
    x = me // (K * Z)
    greet(n, wins, me, y, True)
    greeted(n, wins, True)
    copies = []
    for side, to in ((0, lax.rem(me + n - 1, n)), (1, lax.rem(me + 1, n))):
        copy = pltpu.make_async_remote_copy(
            src_ref=lent.at[side],
            dst_ref=hr.at[side],
            send_sem=sems.at[2 + side],
            recv_sem=sems.at[4 + side],
            device_id=(to, y),
            device_id_type=MESH,
        )
        copy.start()
        copies.append(copy)
    core_copy = pltpu.make_async_remote_copy(
        src_ref=dwc.at[1 - core], dst_ref=core_r, send_sem=rsems.at[0], recv_sem=rsems.at[1],
        device_id=(me + 1 - 2 * core, y), device_id_type=MESH,
    )
    core_copy.start()
    for copy in copies:
        copy.wait()
    gfull[...] = grad[...]
    for t in range(NB):
        gfull[t, 448:512, :] += jnp.where(bnd[1] == t, hr[0], 0.0)
        gfull[t, 0:64, :] += jnp.where(bnd[0] == t, hr[1], 0.0)
    x2s[...] = hilo(gfull[...].reshape(ROWS, C))

    def pick_rows(r, carry):
        idc = column(ids8[r])
        pick = onehot(iota((C, ROWS), 1).astype(f32) == idc)
        rows = fold(dot(pick, x2s[...]))
        per = C // cap
        sbuf[pl.ds(r * per, per)] = rows.reshape(per, cap, C)
        return carry

    lax.fori_loop(0, 8, pick_rows, 0)
    spread(n, me, y, sbuf, rbuf, sems.at[0], sems.at[1])
    rbuf[me] = sbuf[me]
    core_copy.wait()

    def add_core(i, carry):
        xs_[i] = dwc[core, i] + core_r[i]
        return carry

    lax.fori_loop(0, X, add_core, 0)

    def ring(size, at, place_of, src, dst, ssem, rsem):
        def send(o, carry):
            d = lax.rem(at + o, size)
            pltpu.make_async_remote_copy(
                src_ref=src.at[d], dst_ref=dst.at[o - 1], send_sem=ssem, recv_sem=rsem,
                device_id=place_of(d), device_id_type=MESH,
            ).start()
            return carry

        if size > 1:
            lax.fori_loop(1, size, send, 0)
            all_of(size - 1, dst, rsem)
            all_of(size - 1, dst, ssem)

    ring(X, x, lambda d: ((d * Z + z) * K + core, y), xs_, x_r, rsems.at[2], rsems.at[3])

    def add_x(i, carry):
        part = xs_[x, i]
        for o in range(X - 1):
            part = part + x_r[o, i]
        zs_[i] = part
        return carry

    lax.fori_loop(0, Z, add_x, 0)
    ring(Z, z, lambda d: ((x * Z + d) * K + core, y), zs_, z_r, rsems.at[4], rsems.at[5])
    part = zs_[z]
    for o in range(Z - 1):
        part = part + z_r[o]
    ys_[...] = part

    def send_y(o, carry):
        pltpu.make_async_remote_copy(
            src_ref=ys_, dst_ref=y_r.at[o - 1], send_sem=rsems.at[6], recv_sem=rsems.at[7],
            device_id=(me, lax.rem(y + o, wins)), device_id_type=MESH,
        ).start()
        return carry

    lax.fori_loop(1, wins, send_y, 0)
    all_of(wins - 1, y_r, rsems.at[7])
    all_of(wins - 1, y_r, rsems.at[6])
    part = ys_[...]
    for o in range(wins - 1):
        part = part + y_r[o]
    total[...] = part[: chunk_rows(n)]
    all_of(n - 1, rbuf, sems.at[1])
    all_of(n - 1, sbuf, sems.at[0])
    x2s[...] = hilo(rbuf[...].reshape(SLOTS, C))
    pick = onehot(iota((PTS, SLOTS), 1).astype(f32) == column(place[...]))
    pts[...] = fold(dot(pick, x2s[...]))


VM = pl.BlockSpec(memory_space=pltpu.VMEM)
SM = pl.BlockSpec(memory_space=pltpu.SMEM)


def shape(*dims, dtype=f32):
    return jax.ShapeDtypeStruct(dims, dtype)


def middle_call(n, scale, own, halo, cot, wp, nb):
    X, Z, K = PLACES[n]
    return pl.pallas_call(
        functools.partial(middle, n, scale),
        out_shape=(
            shape(NB, 8, 8, 8, C),
            shape(K, X, Z, padded_rows(n), C),
            shape(NB, 8, 8, 8, C),
            shape(2, 8, 8, C),
        ),
        in_specs=[VM] * 4 + [SM],
        out_specs=(VM,) * 4,
        scratch_shapes=[
            pltpu.VMEM((5, 8, 8, 8, C), f32),
            pltpu.VMEM((10, 10, 16, 6 * C), bf16),
            pltpu.VMEM((ROWS, 4 * C), bf16),
            pltpu.VMEM((4, 2 * C, 256), bf16),
            pltpu.VMEM((TAPS * C + 8, C), f32),
            pltpu.VMEM((3, 10, 10, 16, C), f32),
        ],
        compiler_params=pltpu.CompilerParams(vmem_limit_bytes=LIMIT),
        name="middle",
    )(own, halo, cot, wp, nb)


def per_device(n, wins, point_feats, owner_slab, block_slot, voxel_index, boundary, neighbours, weight_taps, cotangent):
    X, Z, K = PLACES[n]
    cap = SLOTS // n
    pad = padded_rows(n)
    bnd = boundary.reshape(2)
    vid = block_slot * VOX + voxel_index
    vis, halo, ids8, place, wp = pl.pallas_call(
        functools.partial(arrive, n, wins),
        out_shape=(shape(ROWS, C), shape(2, 64, C), shape(8, 1, C), shape(1, PTS), shape(TAPS * C, 2 * C, dtype=bf16)),
        in_specs=[VM, VM, VM, SM, VM],
        out_specs=(VM,) * 5,
        scratch_shapes=[
            pltpu.VMEM((n, cap + 1, C), f32),
            pltpu.VMEM((n, cap + 1, C), f32),
            pltpu.VMEM((n, C), f32),
            pltpu.VMEM((SLOTS, 2 * C), bf16),
            pltpu.VMEM((2, 64, C), f32),
            pltpu.VMEM((2, 64, C), f32),
            pltpu.SemaphoreType.DMA((6,)),
        ],
        compiler_params=pltpu.CompilerParams(vmem_limit_bytes=LIMIT, collective_id=0, has_side_effects=True),
        name="arrive",
    )(point_feats[0], owner_slab.reshape(1, PTS), vid, bnd, weight_taps.reshape(TAPS * C, C))
    scale = 1.0 / math.sqrt(wins * n * ROWS)
    act, dwc, grad, lent = middle_call(
        n, scale, vis.reshape(NB, 8, 8, 8, C), halo.reshape(2, 8, 8, C), cotangent.reshape(NB, 8, 8, 8, C), wp, neighbours[0]
    )
    pts, total = pl.pallas_call(
        functools.partial(leave, n, wins),
        out_shape=(shape(PTS, C), shape(chunk_rows(n), C)),
        in_specs=[VM, VM, VM, SM, VM, VM],
        out_specs=(VM,) * 2,
        scratch_shapes=[
            pltpu.VMEM((X, Z, pad, C), f32),
            pltpu.VMEM((X, Z, pad, C), f32),
            pltpu.VMEM((max(X - 1, 1), Z, pad, C), f32),
            pltpu.VMEM((Z, pad, C), f32),
            pltpu.VMEM((max(Z - 1, 1), pad, C), f32),
            pltpu.VMEM((pad, C), f32),
            pltpu.VMEM((max(wins - 1, 1), pad, C), f32),
            pltpu.VMEM((2, 64, C), f32),
            pltpu.VMEM((NB, VOX, C), f32),
            pltpu.VMEM((SLOTS, 2 * C), bf16),
            pltpu.VMEM((n, cap, C), f32),
            pltpu.VMEM((n, cap, C), f32),
            pltpu.SemaphoreType.DMA((6,)),
            pltpu.SemaphoreType.DMA((8,)),
        ],
        compiler_params=pltpu.CompilerParams(vmem_limit_bytes=LIMIT, collective_id=1, has_side_effects=True),
        name="leave",
    )(dwc, grad.reshape(NB, VOX, C), lent.reshape(2, 64, C), bnd, ids8, place)
    return act.reshape(1, ROWS, C), pts[None], total


def solution(mesh):
    n, wins = mesh.shape["slab"], mesh.shape["dp"]
    return jax.shard_map(
        functools.partial(per_device, n, wins),
        mesh=mesh,
        in_specs=(
            P("dp", "slab", None),
            P("dp", "slab", None),
            P("dp", "slab"),
            P("dp", "slab"),
            P("dp", "slab", None, None),
            P("dp", "slab", None),
            P(),
            P("dp", "slab", None),
        ),
        out_specs=(P("dp", "slab", None), P("dp", "slab", None), P("slab", None)),
        check_vma=False,
    )
```

```python
import functools
import math

import jax
import jax.numpy as jnp
from jax import lax
from jax.experimental import pallas as pl
from jax.experimental.pallas import tpu as pltpu
from jax.sharding import PartitionSpec as P

C = 128
E = 8
NB = 2
PTS = 512
VOX = 512
ROWS = NB * VOX
TAPS = 27
SLOTS = 2 * PTS
f32 = jnp.float32
bf16 = jnp.bfloat16
i32 = jnp.int32
MESH = pl.DeviceIdType.MESH
highest = lax.Precision.HIGHEST
LIMIT = 60 * 1024 * 1024
PLACES = {64: (4, 8, 2), 8: (2, 2, 2), 4: (2, 1, 2)}


def iota(shape, dim):
    return lax.broadcasted_iota(i32, shape, dim)


def split(v):
    hi = v.astype(bf16)
    return hi, (v - hi.astype(f32)).astype(bf16)


def hilo(v):
    return jnp.concatenate(split(v), axis=-1)


def onehot(where):
    return jnp.where(where, 1.0, 0.0).astype(bf16)


def fold(v):
    return v[:, :C] + v[:, C:]


def dot(a, b):
    return lax.dot_general(a, b, (((1,), (0,)), ((), ())), preferred_element_type=f32)


def column(row):
    return jnp.transpose(jnp.broadcast_to(row, (8, row.shape[1])))[:, 0:1]


def pack_points(n, me, feats, own, slot, vox, sbuf, place, idrows):
    cap = SLOTS // n
    group = C // cap
    ownr = own[...].astype(f32)
    ownc = column(ownr)
    first = iota((PTS, PTS), 0) < iota((PTS, PTS), 1)
    same = (ownc == ownr) & first
    rank = jnp.sum(jnp.where(same, 1.0, 0.0), axis=0, keepdims=True)
    placed = ownr * cap + rank
    place[...] = placed
    x2 = hilo(feats[...])
    pick = onehot(iota((SLOTS, PTS), 0).astype(f32) == placed)
    rows = fold(dot(pick, x2))
    sbuf[:, 0:cap, :] = rows.reshape(n, cap, C)
    lane = iota((PTS, C), 1).astype(f32)
    shift = (lax.rem(me, group) * cap).astype(f32)
    to_lane = jnp.where(lane == column(rank) + shift, 1.0, 0.0)
    ids = (slot[...] * VOX + vox[...]).astype(f32) + 1.0
    to_dest = jnp.where(iota((n, PTS), 0).astype(f32) == ownr, ids, 0.0)
    idrows[...] = lax.dot_general(
        to_dest, to_lane, (((1,), (0,)), ((), ())), precision=highest, preferred_element_type=f32
    )

    def put(d, carry):
        sbuf[d, cap : cap + 1, :] = idrows[pl.ds(d, 1), :]
        return carry

    lax.fori_loop(0, n, put, 0)


def prepare_taps(w, wp):
    def step(t, carry):
        rows = pl.ds(pl.multiple_of(t * 384, 384), 384)
        wp[rows, :] = hilo(w[rows, :])
        return carry

    lax.fori_loop(0, 9, step, 0)


def voxelize(n, rbuf, ids8, x2s, vis):
    cap = SLOTS // n
    group = C // cap
    x2s[...] = hilo(rbuf[:, 0:cap, :].reshape(SLOTS, C))
    ids = rbuf[:, cap : cap + 1, :].reshape(8, group, 1, C).sum(axis=1)
    ids8[...] = ids - 1.0

    def step(t, carry):
        vox = (iota((256, C), 0) + t * 256).astype(f32)
        pick = jnp.concatenate([onehot(vox == ids8[r]) for r in range(8)], axis=1)
        vis[t // 2, pl.ds(lax.rem(t, 2) * 4, 4)] = fold(dot(pick, x2s[...])).reshape(4, 8, 8, C)
        return carry

    lax.fori_loop(0, 4, step, 0)


SEC_P = ((slice(0, 1), slice(7, 8)), (slice(1, 9), slice(0, 8)), (slice(9, 10), slice(0, 1)))


def sections(which=(0, 1, 2)):
    for i in which:
        for j in range(3):
            if i == 1 and j == 1:
                for p in range(8):
                    yield i, j, slice(p + 1, p + 2), slice(1, 9), slice(p, p + 1), slice(0, 8)
            else:
                (ps, xs), (qs, ys) = SEC_P[i], SEC_P[j]
                yield i, j, ps, qs, xs, ys


def build_windows(nb, vis, S, which):
    for i, j, ps, qs, xs, ys in sections(which):
        e = 9 * i + 3 * j
        parts = ([], [], [])
        for b in range(NB):
            mid = vis[nb[b, e + 1], xs, ys]
            low = vis[nb[b, e], xs, ys]
            high = vis[nb[b, e + 2], xs, ys]
            z = iota(mid.shape, 2)
            parts[0].append(jnp.roll(jnp.where(z == 7, low, mid), 1, axis=2))
            parts[1].append(mid)
            parts[2].append(jnp.roll(jnp.where(z == 0, high, mid), -1, axis=2))
        for k in range(3):
            hi, lo = split(jnp.concatenate(parts[k], axis=2))
            S[ps, qs, :, k * C : (k + 1) * C] = hi
            S[ps, qs, :, (3 + k) * C : (4 + k) * C] = lo


def forward(S, wp, cot, act, G4, GT):
    def step(m, carry):
        total = None
        for part in range(2):
            wins = []
            for i in range(3):
                for j in range(3):
                    win = S[pl.ds(2 * m + i, 2), j : j + 8, :, part * 384 : part * 384 + 384]
                    wins.append(win.reshape(256, 384))
            got = dot(jnp.concatenate(wins, axis=1), wp[...])
            total = got if total is None else total + got
        pre = fold(total).reshape(2, 8, 16, C)
        gate = 1.0 / (1.0 + jnp.exp(-pre))
        xs = pl.ds(2 * m, 2)
        out = pre * gate
        for b in range(NB):
            act[b, xs] = out[:, :, 8 * b : 8 * b + 8]
        up = jnp.concatenate([cot[b, xs] for b in range(NB)], axis=2)
        g = (up * gate * (1.0 + pre * (1.0 - gate))).reshape(256, C)
        hi, lo = split(g)
        rows = pl.ds(pl.multiple_of(256 * m, 256), 256)
        G4[rows, :] = jnp.concatenate([hi, hi, lo, lo], axis=1)
        gt = jnp.transpose(g)
        thi, tlo = split(gt)
        GT[m, 0:C, :] = thi
        GT[m, C : 2 * C, :] = tlo
        return carry

    lax.fori_loop(0, 4, step, 0)


def weight_grad(S, GT, dW, scale):
    def step(ij, carry):
        i, j = ij // 3, lax.rem(ij, 3)
        total = None
        for m in range(4):
            win = S[pl.ds(i + 2 * m, 2), pl.ds(j, 8)].reshape(256, 768)
            got = dot(GT[m], win)
            total = got if total is None else total + got
        both = total[:C] + total[C:]
        for k in range(3):
            one = both[:, k * C : (k + 1) * C] + both[:, (3 + k) * C : (4 + k) * C]
            rows = pl.ds(pl.multiple_of(ij * 384 + k * C, C), C)
            dW[rows, :] = jnp.transpose(one) * scale
        return carry

    lax.fori_loop(0, 9, step, 0)


def input_grad(G4, wp, A, first, last):
    if first == 0:
        A[...] = jnp.zeros_like(A)

    def step(ij, carry):
        i, j = ij // 3, lax.rem(ij, 3)
        w = wp[pl.ds(pl.multiple_of(ij * 384, 384), 384), :]
        w2 = jnp.concatenate([w, w], axis=1)
        for m in range(4):
            y = lax.dot_general(
                G4[m * 256 : (m + 1) * 256, :], w2, (((1,), (1,)), ((), ())), preferred_element_type=f32
            )
            for k in range(3):
                A[k, pl.ds(i + 2 * m, 2), pl.ds(j, 8)] += y[:, k * C : (k + 1) * C].reshape(2, 8, 16, C)
        return carry

    lax.fori_loop(first, last, step, 0)


def carry_back(nb, A, grad, lent):
    grad[...] = jnp.zeros_like(grad)
    lent[...] = jnp.zeros_like(lent)
    for i, j, ps, qs, xs, ys in sections():
        e = 9 * i + 3 * j
        for b in range(NB):
            a0, a1, a2 = (A[k, ps, qs, 8 * b : 8 * b + 8, :] for k in range(3))
            z = iota(a0.shape, 2)
            a0 = jnp.roll(a0, -1, axis=2)
            a2 = jnp.roll(a2, 1, axis=2)
            mid = a1 + jnp.where(z == 7, 0.0, a0) + jnp.where(z == 0, 0.0, a2)
            low = jnp.where(z == 7, a0, 0.0)
            high = jnp.where(z == 0, a2, 0.0)

            def share(t):
                part = jnp.where(nb[b, e] == t, low, 0.0) + jnp.where(nb[b, e + 2] == t, high, 0.0)
                if i == 1 and j == 1:
                    return part + mid if t == b else part
                return part + jnp.where(nb[b, e + 1] == t, mid, 0.0)

            for t in range(NB):
                grad[t, xs, ys] += share(t)
            if i == 0:
                lent[0, ys] += share(2)[0]
            if i == 2:
                lent[1, ys] += share(3)[0]


def chunk_rows(n):
    return TAPS * C // n


def padded_rows(n):
    return -(-chunk_rows(n) // 8) * 8


def cut_chunks(n, dW, dwc):
    X, Z, K = PLACES[n]
    size, pad = chunk_rows(n), padded_rows(n)
    for d in range(n):
        dwc[d % K, d // K // Z, d // K % Z] = dW[size * d : size * d + pad, :]


def greet(n, wins, me, y, columns):
    barrier = pltpu.get_barrier_semaphore()

    def hello(o, carry):
        pl.semaphore_signal(barrier, inc=1, device_id=(lax.rem(me + o, n), y), device_id_type=MESH)
        return carry

    lax.fori_loop(1, n, hello, 0)
    if columns:

        def hello_y(o, carry):
            pl.semaphore_signal(barrier, inc=1, device_id=(me, lax.rem(y + o, wins)), device_id_type=MESH)
            return carry

        lax.fori_loop(1, wins, hello_y, 0)


def greeted(n, wins, columns):
    pl.semaphore_wait(pltpu.get_barrier_semaphore(), n - 1 + (wins - 1 if columns else 0))


def spread(n, me, y, src, dst, ssem, rsem):
    def send(o, carry):
        d = lax.rem(me + o, n)
        pltpu.make_async_remote_copy(
            src_ref=src.at[d], dst_ref=dst.at[me], send_sem=ssem, recv_sem=rsem, device_id=(d, y), device_id_type=MESH
        ).start()
        return carry

    lax.fori_loop(1, n, send, 0)


def all_of(count, ref, sem):
    pltpu.make_async_copy(ref.at[pl.ds(0, count)], ref.at[pl.ds(0, count)], sem).wait()

def both_ways(n, me, y, src, dst, sems, turn):
    copies = []
    for side in range(2):
        step = 1 if (side == 0) != turn else n - 1
        copy = pltpu.make_async_remote_copy(
            src_ref=src.at[side],
            dst_ref=dst.at[side],
            send_sem=sems.at[side],
            recv_sem=sems.at[2 + side],
            device_id=(lax.rem(me + step, n), y),
            device_id_type=MESH,
        )
        copy.start()
        copies.append(copy)
    return copies


def whole(
    n, wins, scale,
    feats, own, slot, vox, bnd, nb, w, cot,
    act, back, place, parts,
    sbuf, rbuf, idrows, ids8, x2s, vis, hs, hr, wp, S, G4, GT, dW, A, grad, lent, lent_r, bbuf,
    dwc, core_r, xs_, x_r, zs_, z_r, psems, hsems, bsems, qsems, rsems,
):
    X, Z, K = PLACES[n]
    cap = SLOTS // n
    me, y = lax.axis_index("slab"), lax.axis_index("dp")
    core = lax.rem(me, K)
    z = lax.rem(me // K, Z)
    x = me // (K * Z)
    greet(n, wins, me, y, True)
    pack_points(n, me, feats, own, slot, vox, sbuf, place, idrows)
    greeted(n, wins, True)
    spread(n, me, y, sbuf, rbuf, psems.at[0], psems.at[1])
    rbuf[me] = sbuf[me]
    prepare_taps(w, wp)
    vis[4] = jnp.zeros((8, 8, 8, C), f32)
    all_of(n - 1, rbuf, psems.at[1])
    voxelize(n, rbuf, ids8, x2s, vis)
    hs[0] = jnp.where(bnd[1] == 1, vis[1, 7], vis[0, 7])
    hs[1] = jnp.where(bnd[0] == 1, vis[1, 0], vis[0, 0])
    copies = both_ways(n, me, y, hs, hr, hsems, False)
    build_windows(nb, vis, S, (1,))
    all_of(n - 1, sbuf, psems.at[0])
    for copy in copies:
        copy.wait()
    vis[2, 7] = hr[0]
    vis[3, 0] = hr[1]
    build_windows(nb, vis, S, (0, 2))
    forward(S, wp, cot, act, G4, GT)
    weight_grad(S, GT, dW, scale)
    cut_chunks(n, dW, dwc)
    core_copy = pltpu.make_async_remote_copy(
        src_ref=dwc.at[1 - core], dst_ref=core_r, send_sem=rsems.at[0], recv_sem=rsems.at[1],
        device_id=(me + 1 - 2 * core, y), device_id_type=MESH,
    )
    core_copy.start()
    input_grad(G4, wp, A, 0, 4)
    core_copy.wait()

    def add_core(i, carry):
        xs_[i] = dwc[core, i] + core_r[i]
        return carry

    lax.fori_loop(0, X, add_core, 0)

    def ring(size, at, place_of, src, dst, ssem, rsem):
        def send(o, carry):
            d = lax.rem(at + o, size)
            pltpu.make_async_remote_copy(
                src_ref=src.at[d], dst_ref=dst.at[o - 1], send_sem=ssem, recv_sem=rsem,
                device_id=place_of(d), device_id_type=MESH,
            ).start()
            return carry

        if size > 1:
            lax.fori_loop(1, size, send, 0)

    def ring_done(size, dst, ssem, rsem):
        if size > 1:
            all_of(size - 1, dst, rsem)
            all_of(size - 1, dst, ssem)

    ring(X, x, lambda d: ((d * Z + z) * K + core, y), xs_, x_r, rsems.at[2], rsems.at[3])
    input_grad(G4, wp, A, 4, 9)
    carry_back(nb, A, grad, lent)
    copies = both_ways(n, me, y, lent, lent_r, bsems, True)
    for copy in copies:
        copy.wait()
    for t in range(NB):
        grad[t, 7] += jnp.where(bnd[1] == t, lent_r[0], 0.0)
        grad[t, 0] += jnp.where(bnd[0] == t, lent_r[1], 0.0)
    x2s[...] = hilo(grad[...].reshape(ROWS, C))

    def pick_rows(r, carry):
        pick = onehot(iota((C, ROWS), 1).astype(f32) == column(ids8[r]))
        per = C // cap
        bbuf[pl.ds(r * per, per)] = fold(dot(pick, x2s[...])).reshape(per, cap, C)
        return carry

    lax.fori_loop(0, 8, pick_rows, 0)
    spread(n, me, y, bbuf, back, qsems.at[0], qsems.at[1])
    back[me] = bbuf[me]
    ring_done(X, x_r, rsems.at[2], rsems.at[3])

    def add_x(i, carry):
        part = xs_[x, i]
        for o in range(X - 1):
            part = part + x_r[o, i]
        zs_[i] = part
        return carry

    lax.fori_loop(0, Z, add_x, 0)
    ring(Z, z, lambda d: ((x * Z + d) * K + core, y), zs_, z_r, rsems.at[4], rsems.at[5])
    ring_done(Z, z_r, rsems.at[4], rsems.at[5])
    part = zs_[z]
    for o in range(Z - 1):
        part = part + z_r[o]
    parts[wins - 1] = part

    def send_y(o, carry):
        pltpu.make_async_remote_copy(
            src_ref=parts.at[wins - 1], dst_ref=parts.at[o - 1], send_sem=rsems.at[6], recv_sem=rsems.at[7],
            device_id=(me, lax.rem(y + o, wins)), device_id_type=MESH,
        ).start()
        return carry

    lax.fori_loop(1, wins, send_y, 0)
    all_of(n - 1, back, qsems.at[1])
    all_of(n - 1, bbuf, qsems.at[0])
    all_of(wins - 1, parts, rsems.at[7])
    all_of(wins - 1, parts, rsems.at[6])


def finish(n, wins, act_in, back, place, parts, act, pts, total):
    act[...] = act_in[...]
    part = parts[0]
    for o in range(1, wins):
        part = part + parts[o]
    total[...] = part[: chunk_rows(n)]
    rows = hilo(back[...].reshape(SLOTS, C))
    pick = onehot(iota((PTS, SLOTS), 1).astype(f32) == column(place[...]))
    pts[...] = fold(dot(pick, rows))


VM = pl.BlockSpec(memory_space=pltpu.VMEM)
SM = pl.BlockSpec(memory_space=pltpu.SMEM)


def shape(*dims, dtype=f32):
    return jax.ShapeDtypeStruct(dims, dtype)


def per_device(n, wins, point_feats, owner_slab, block_slot, voxel_index, boundary, neighbours, weight_taps, cotangent):
    X, Z, K = PLACES[n]
    cap = SLOTS // n
    pad = padded_rows(n)
    scale = 1.0 / math.sqrt(wins * n * ROWS)
    vm = pltpu.VMEM
    dma = pltpu.SemaphoreType.DMA
    act, back, place, parts = pl.pallas_call(
        functools.partial(whole, n, wins, scale),
        out_shape=(shape(NB, 8, 8, 8, C), shape(n, cap, C), shape(1, PTS), shape(wins, pad, C)),
        in_specs=[VM, VM, VM, VM, SM, SM, VM, VM],
        out_specs=(VM,) * 4,
        scratch_shapes=[
            vm((n, cap + 1, C), f32),
            vm((n, cap + 1, C), f32),
            vm((n, C), f32),
            vm((8, 1, C), f32),
            vm((SLOTS, 2 * C), bf16),
            vm((5, 8, 8, 8, C), f32),
            vm((2, 8, 8, C), f32),
            vm((2, 8, 8, C), f32),
            vm((TAPS * C, 2 * C), bf16),
            vm((10, 10, 16, 6 * C), bf16),
            vm((ROWS, 4 * C), bf16),
            vm((4, 2 * C, 256), bf16),
            vm((TAPS * C + 8, C), f32),
            vm((3, 10, 10, 16, C), f32),
            vm((NB, 8, 8, 8, C), f32),
            vm((2, 8, 8, C), f32),
            vm((2, 8, 8, C), f32),
            vm((n, cap, C), f32),
            vm((K, X, Z, pad, C), f32),
            vm((X, Z, pad, C), f32),
            vm((X, Z, pad, C), f32),
            vm((max(X - 1, 1), Z, pad, C), f32),
            vm((Z, pad, C), f32),
            vm((max(Z - 1, 1), pad, C), f32),
            dma((2,)),
            dma((4,)),
            dma((4,)),
            dma((2,)),
            dma((8,)),
        ],
        compiler_params=pltpu.CompilerParams(vmem_limit_bytes=LIMIT, collective_id=0, has_side_effects=True),
        name="whole",
    )(
        point_feats[0],
        owner_slab.reshape(1, PTS),
        block_slot,
        voxel_index,
        boundary.reshape(2),
        neighbours[0],
        weight_taps.reshape(TAPS * C, C),
        cotangent.reshape(NB, 8, 8, 8, C),
    )
    act, pts, total = pl.pallas_call(
        functools.partial(finish, n, wins),
        out_shape=(shape(ROWS, C), shape(PTS, C), shape(chunk_rows(n), C)),
        in_specs=[VM] * 4,
        out_specs=(VM,) * 3,
        compiler_params=pltpu.CompilerParams(vmem_limit_bytes=LIMIT),
        name="finish",
    )(act.reshape(ROWS, C), back, place, parts)
    return act[None], pts[None], total


def solution(mesh):
    n, wins = mesh.shape["slab"], mesh.shape["dp"]
    return jax.shard_map(
        functools.partial(per_device, n, wins),
        mesh=mesh,
        in_specs=(
            P("dp", "slab", None),
            P("dp", "slab", None),
            P("dp", "slab"),
            P("dp", "slab"),
            P("dp", "slab", None, None),
            P("dp", "slab", None),
            P(),
            P("dp", "slab", None),
        ),
        out_specs=(P("dp", "slab", None), P("dp", "slab", None), P("slab", None)),
        check_vma=False,
    )
```

```python
import functools
import math

import jax
import jax.numpy as jnp
from jax import lax
from jax.experimental import pallas as pl
from jax.experimental.pallas import tpu as pltpu
from jax.sharding import PartitionSpec as P

C = 128
E = 8
NB = 2
PTS = 512
VOX = 512
ROWS = NB * VOX
TAPS = 27
SLOTS = 2 * PTS
f32 = jnp.float32
bf16 = jnp.bfloat16
i32 = jnp.int32
MESH = pl.DeviceIdType.MESH
highest = lax.Precision.HIGHEST
LIMIT = 60 * 1024 * 1024
PLACES = {64: (4, 8, 2), 8: (2, 2, 2), 4: (2, 1, 2)}


def iota(shape, dim):
    return lax.broadcasted_iota(i32, shape, dim)


def split(v):
    hi = v.astype(bf16)
    return hi, (v - hi.astype(f32)).astype(bf16)


def hilo(v):
    return jnp.concatenate(split(v), axis=-1)


def onehot(where):
    return jnp.where(where, 1.0, 0.0).astype(bf16)


def fold(v):
    return v[:, :C] + v[:, C:]


def dot(a, b):
    return lax.dot_general(a, b, (((1,), (0,)), ((), ())), preferred_element_type=f32)


def column(row):
    return jnp.transpose(jnp.broadcast_to(row, (8, row.shape[1])))[:, 0:1]


def pack_points(n, me, feats, own, slot, vox, sbuf, place, idrows):
    cap = SLOTS // n
    group = C // cap
    ownr = own[...].astype(f32)
    ownc = column(ownr)
    first = iota((PTS, PTS), 0) < iota((PTS, PTS), 1)
    same = (ownc == ownr) & first
    rank = jnp.sum(jnp.where(same, 1.0, 0.0), axis=0, keepdims=True)
    placed = ownr * cap + rank
    place[...] = placed
    x2 = hilo(feats[...])
    pick = onehot(iota((SLOTS, PTS), 0).astype(f32) == placed)
    rows = fold(dot(pick, x2))
    sbuf[:, 0:cap, :] = rows.reshape(n, cap, C)
    lane = iota((PTS, C), 1).astype(f32)
    shift = (lax.rem(me, group) * cap).astype(f32)
    to_lane = jnp.where(lane == column(rank) + shift, 1.0, 0.0)
    ids = (slot[...] * VOX + vox[...]).astype(f32) + 1.0
    to_dest = jnp.where(iota((n, PTS), 0).astype(f32) == ownr, ids, 0.0)
    idrows[...] = lax.dot_general(
        to_dest, to_lane, (((1,), (0,)), ((), ())), precision=highest, preferred_element_type=f32
    )

    def put(d, carry):
        sbuf[d, cap : cap + 1, :] = idrows[pl.ds(d, 1), :]
        return carry

    lax.fori_loop(0, n, put, 0)


def prepare_taps(w, wp):
    def step(t, carry):
        rows = pl.ds(pl.multiple_of(t * 384, 384), 384)
        wp[rows, :] = hilo(w[rows, :])
        return carry

    lax.fori_loop(0, 9, step, 0)


def voxelize(n, rbuf, ids8, x2s, vis):
    cap = SLOTS // n
    group = C // cap
    x2s[...] = hilo(rbuf[:, 0:cap, :].reshape(SLOTS, C))
    ids = rbuf[:, cap : cap + 1, :].reshape(8, group, 1, C).sum(axis=1)
    ids8[...] = ids - 1.0

    def step(t, carry):
        vox = (iota((256, C), 0) + t * 256).astype(f32)
        pick = jnp.concatenate([onehot(vox == ids8[r]) for r in range(8)], axis=1)
        vis[t // 2, pl.ds(lax.rem(t, 2) * 4, 4)] = fold(dot(pick, x2s[...])).reshape(4, 8, 8, C)
        return carry

    lax.fori_loop(0, 4, step, 0)


SEC_P = ((slice(0, 1), slice(7, 8)), (slice(1, 9), slice(0, 8)), (slice(9, 10), slice(0, 1)))


def sections(which=(0, 1, 2)):
    for i in which:
        for j in range(3):
            if i == 1 and j == 1:
                for p in range(8):
                    yield i, j, slice(p + 1, p + 2), slice(1, 9), slice(p, p + 1), slice(0, 8)
            else:
                (ps, xs), (qs, ys) = SEC_P[i], SEC_P[j]
                yield i, j, ps, qs, xs, ys


def build_windows(nb, vis, S, which):
    for i, j, ps, qs, xs, ys in sections(which):
        e = 9 * i + 3 * j
        parts = ([], [], [])
        for b in range(NB):
            mid = vis[nb[b, e + 1], xs, ys]
            low = vis[nb[b, e], xs, ys]
            high = vis[nb[b, e + 2], xs, ys]
            z = iota(mid.shape, 2)
            parts[0].append(jnp.roll(jnp.where(z == 7, low, mid), 1, axis=2))
            parts[1].append(mid)
            parts[2].append(jnp.roll(jnp.where(z == 0, high, mid), -1, axis=2))
        for k in range(3):
            hi, lo = split(jnp.concatenate(parts[k], axis=2))
            S[ps, qs, :, k * C : (k + 1) * C] = hi
            S[ps, qs, :, (3 + k) * C : (4 + k) * C] = lo


def forward(S, wp, cot, act, G4, GT):
    def step(m, carry):
        total = None
        for part in range(2):
            wins = []
            for i in range(3):
                for j in range(3):
                    win = S[pl.ds(2 * m + i, 2), j : j + 8, :, part * 384 : part * 384 + 384]
                    wins.append(win.reshape(256, 384))
            got = dot(jnp.concatenate(wins, axis=1), wp[...])
            total = got if total is None else total + got
        pre = fold(total).reshape(2, 8, 16, C)
        gate = 1.0 / (1.0 + jnp.exp(-pre))
        xs = pl.ds(2 * m, 2)
        out = pre * gate
        for b in range(NB):
            act[b, xs] = out[:, :, 8 * b : 8 * b + 8]
        up = jnp.concatenate([cot[b, xs] for b in range(NB)], axis=2)
        g = (up * gate * (1.0 + pre * (1.0 - gate))).reshape(256, C)
        hi, lo = split(g)
        rows = pl.ds(pl.multiple_of(256 * m, 256), 256)
        G4[rows, :] = jnp.concatenate([hi, hi, lo, lo], axis=1)
        gt = jnp.transpose(g)
        thi, tlo = split(gt)
        GT[m, 0:C, :] = thi
        GT[m, C : 2 * C, :] = tlo
        return carry

    lax.fori_loop(0, 4, step, 0)


def weight_grad(S, GT, dW, scale, first, last):
    def step(ij, carry):
        i, j = ij // 3, lax.rem(ij, 3)
        total = None
        for m in range(4):
            win = S[pl.ds(i + 2 * m, 2), pl.ds(j, 8)].reshape(256, 768)
            got = dot(GT[m], win)
            total = got if total is None else total + got
        both = total[:C] + total[C:]
        for k in range(3):
            one = both[:, k * C : (k + 1) * C] + both[:, (3 + k) * C : (4 + k) * C]
            rows = pl.ds(pl.multiple_of(ij * 384 + k * C, C), C)
            dW[rows, :] = jnp.transpose(one) * scale
        return carry

    lax.fori_loop(first, last, step, 0)


def input_grad(G4, wp, A, first, last):
    if first == 0:
        A[...] = jnp.zeros_like(A)

    def some(ij, count):
        size = 384 * count
        w = wp[pl.ds(pl.multiple_of(ij * 384, 384), size), :]
        w2 = jnp.concatenate([w, w], axis=1)
        for m in range(4):
            y = lax.dot_general(
                G4[m * 256 : (m + 1) * 256, :], w2, (((1,), (1,)), ((), ())), preferred_element_type=f32
            )
            for c in range(count):
                i, j = (ij + c) // 3, lax.rem(ij + c, 3)
                for k in range(3):
                    col = (3 * c + k) * C
                    A[k, pl.ds(i + 2 * m, 2), pl.ds(j, 8)] += y[:, col : col + C].reshape(2, 8, 16, C)

    def step(p, carry):
        some(first + 2 * p, 2)
        return carry

    lax.fori_loop(0, (last - first) // 2, step, 0)
    if (last - first) % 2:
        some(last - 1, 1)


def carry_back(nb, A, grad, lent):
    grad[...] = jnp.zeros_like(grad)
    lent[...] = jnp.zeros_like(lent)
    for i, j, ps, qs, xs, ys in sections():
        e = 9 * i + 3 * j
        for b in range(NB):
            a0, a1, a2 = (A[k, ps, qs, 8 * b : 8 * b + 8, :] for k in range(3))
            z = iota(a0.shape, 2)
            a0 = jnp.roll(a0, -1, axis=2)
            a2 = jnp.roll(a2, 1, axis=2)
            mid = a1 + jnp.where(z == 7, 0.0, a0) + jnp.where(z == 0, 0.0, a2)
            low = jnp.where(z == 7, a0, 0.0)
            high = jnp.where(z == 0, a2, 0.0)

            def share(t):
                part = jnp.where(nb[b, e] == t, low, 0.0) + jnp.where(nb[b, e + 2] == t, high, 0.0)
                if i == 1 and j == 1:
                    return part + mid if t == b else part
                return part + jnp.where(nb[b, e + 1] == t, mid, 0.0)

            for t in range(NB):
                grad[t, xs, ys] += share(t)
            if i == 0:
                lent[0, ys] += share(2)[0]
            if i == 2:
                lent[1, ys] += share(3)[0]


def chunk_rows(n):
    return TAPS * C // n


def padded_rows(n):
    return -(-chunk_rows(n) // 8) * 8


def cut_chunks(n, dW, dwc, first, last):
    X, Z, K = PLACES[n]
    size, pad = chunk_rows(n), padded_rows(n)
    for d in range(first, last):
        dwc[d % K, d // K // Z, d // K % Z] = dW[size * d : size * d + pad, :]


def holders(n, wins):
    tiles = padded_rows(n) // 8
    return max(h for h in range(1, wins + 1) if tiles % h == 0)


def greet(n, wins, me, y):
    X, Z, K = PLACES[n]
    core, z, x = lax.rem(me, K), lax.rem(me // K, Z), me // (K * Z)
    barrier = pltpu.get_barrier_semaphore()

    def hello(o, carry):
        pl.semaphore_signal(barrier, inc=1, device_id=(lax.rem(me + o, n), y), device_id_type=MESH)
        return carry

    lax.fori_loop(1, n, hello, 0)

    def hello_y(o, carry):
        to = (x * Z + lax.rem(o, Z)) * K + core
        pl.semaphore_signal(barrier, inc=1, device_id=(to, lax.rem(y + 1 + o // Z, wins)), device_id_type=MESH)
        return carry

    lax.fori_loop(0, Z * (wins - 1), hello_y, 0)


def greeted(n, wins):
    pl.semaphore_wait(pltpu.get_barrier_semaphore(), n - 1 + PLACES[n][1] * (wins - 1))


def spread(n, me, y, src, dst, ssem, rsem):
    def send(o, carry):
        d = lax.rem(me + o, n)
        pltpu.make_async_remote_copy(
            src_ref=src.at[d], dst_ref=dst.at[me], send_sem=ssem, recv_sem=rsem, device_id=(d, y), device_id_type=MESH
        ).start()
        return carry

    lax.fori_loop(1, n, send, 0)


def all_of(count, ref, sem):
    pltpu.make_async_copy(ref.at[pl.ds(0, count)], ref.at[pl.ds(0, count)], sem).wait()

def both_ways(n, me, y, src, dst, sems, turn):
    copies = []
    for side in range(2):
        step = 1 if (side == 0) != turn else n - 1
        copy = pltpu.make_async_remote_copy(
            src_ref=src.at[side],
            dst_ref=dst.at[side],
            send_sem=sems.at[side],
            recv_sem=sems.at[2 + side],
            device_id=(lax.rem(me + step, n), y),
            device_id_type=MESH,
        )
        copy.start()
        copies.append(copy)
    return copies


def whole(
    n, wins, scale,
    feats, own, slot, vox, bnd, nb, w_in, cot_in,
    act_out, back, place, tot,
    w, cot, act, sbuf, rbuf, idrows, ids8, x2s, vis, hs, hr, wp, S, G4, GT, dW, A, grad, lent, lent_r, bbuf,
    dwc, core_r, xs_, x_r, zs_, zy_r, lsems, psems, hsems, bsems, qsems, csems, rsems,
):
    X, Z, K = PLACES[n]
    cap = SLOTS // n
    held = holders(n, wins)
    me, y = lax.axis_index("slab"), lax.axis_index("dp")
    core = lax.rem(me, K)
    z = lax.rem(me // K, Z)
    x = me // (K * Z)

    def remote(src, dst, ssem, rsem, slab, win):
        return pltpu.make_async_remote_copy(
            src_ref=src, dst_ref=dst, send_sem=ssem, recv_sem=rsem, device_id=(slab, win), device_id_type=MESH
        )

    w_copy = pltpu.make_async_copy(w_in, w, lsems.at[0])
    cot_copy = pltpu.make_async_copy(cot_in, cot, lsems.at[1])
    w_copy.start()
    cot_copy.start()
    greet(n, wins, me, y)
    pack_points(n, me, feats, own, slot, vox, sbuf, place, idrows)
    greeted(n, wins)
    spread(n, me, y, sbuf, rbuf, psems.at[0], psems.at[1])
    rbuf[me] = sbuf[me]
    vis[4] = jnp.zeros((8, 8, 8, C), f32)
    w_copy.wait()
    cot_copy.wait()
    prepare_taps(w, wp)
    all_of(n - 1, rbuf, psems.at[1])
    voxelize(n, rbuf, ids8, x2s, vis)
    hs[0] = jnp.where(bnd[1] == 1, vis[1, 7], vis[0, 7])
    hs[1] = jnp.where(bnd[0] == 1, vis[1, 0], vis[0, 0])
    copies = both_ways(n, me, y, hs, hr, hsems, False)
    build_windows(nb, vis, S, (1,))
    all_of(n - 1, sbuf, psems.at[0])
    for copy in copies:
        copy.wait()
    vis[2, 7] = hr[0]
    vis[3, 0] = hr[1]
    build_windows(nb, vis, S, (0, 2))
    forward(S, wp, cot, act, G4, GT)
    act_copy = pltpu.make_async_copy(act, act_out, lsems.at[2])
    act_copy.start()

    wide = X // 2

    def half_of(h):
        return pl.ds(h * wide, wide)

    def core_start(h):
        cut_chunks(n, dW, dwc, h * n // 2, (h + 1) * n // 2)
        copy = remote(
            dwc.at[1 - core, half_of(h)], core_r.at[half_of(h)], csems.at[h], csems.at[2 + h], me + 1 - 2 * core, y
        )
        copy.start()
        return copy

    def core_add(h):
        def add_core(i, carry):
            xs_[i] = dwc[core, i] + core_r[i]
            return carry

        lax.fori_loop(h * wide, (h + 1) * wide, add_core, 0)

    def x_start(h):
        def send(o, carry):
            d = lax.rem(x + o, X)

            @pl.when(d // wide == h)
            def _():
                remote(xs_.at[d], x_r.at[o - 1], rsems.at[0], rsems.at[1], (d * Z + z) * K + core, y).start()

            return carry

        lax.fori_loop(1, X, send, 0)

    weight_grad(S, GT, dW, scale, 0, 5)
    core_0 = core_start(0)
    weight_grad(S, GT, dW, scale, 5, 9)
    core_0.wait()
    core_add(0)
    x_start(0)
    core_1 = core_start(1)
    input_grad(G4, wp, A, 0, 4)
    core_1.wait()
    core_add(1)
    x_start(1)
    input_grad(G4, wp, A, 4, 9)
    carry_back(nb, A, grad, lent)
    copies = both_ways(n, me, y, lent, lent_r, bsems, True)
    all_of(X - 1, x_r, rsems.at[1])
    all_of(X - 1, x_r, rsems.at[0])

    def add_x(i, carry):
        part = xs_[x, i]
        for o in range(X - 1):
            part = part + x_r[o, i]
        zs_[i] = part.reshape(zs_.shape[1:])
        return carry

    lax.fori_loop(0, Z, add_x, 0)

    def send_zy(o, carry):
        zd, yd = lax.rem(z + o // held, Z), lax.rem(o, held)

        @pl.when((o >= held) | (yd != y))
        def _():
            remote(
                zs_.at[zd, yd], zy_r.at[z * wins + y], rsems.at[2], rsems.at[3], (x * Z + zd) * K + core, yd
            ).start()

        return carry

    lax.fori_loop(0, Z * held, send_zy, 0)
    for copy in copies:
        copy.wait()
    for t in range(NB):
        grad[t, 7] += jnp.where(bnd[1] == t, lent_r[0], 0.0)
        grad[t, 0] += jnp.where(bnd[0] == t, lent_r[1], 0.0)
    x2s[...] = hilo(grad[...].reshape(ROWS, C))

    def pick_rows(r, carry):
        pick = onehot(iota((C, ROWS), 1).astype(f32) == column(ids8[r]))
        per = C // cap
        bbuf[pl.ds(r * per, per)] = fold(dot(pick, x2s[...])).reshape(per, cap, C)
        return carry

    lax.fori_loop(0, 8, pick_rows, 0)
    spread(n, me, y, bbuf, back, qsems.at[0], qsems.at[1])
    back[me] = bbuf[me]

    @pl.when(y < held)
    def _():
        all_of(Z * wins - 1, zy_r, rsems.at[3])
        zy_r[z * wins + y] = zs_[z, y]

        def add_piece(o, part):
            return part + zy_r[o]

        tot[y] = lax.fori_loop(1, Z * wins, add_piece, zy_r[0])

        def send_y(o, carry):
            remote(tot.at[y], tot.at[y], rsems.at[4], rsems.at[5], me, lax.rem(y + o, wins)).start()
            return carry

        lax.fori_loop(1, wins, send_y, 0)

    @pl.when(y < held)
    def _():
        all_of(Z * held - 1, zy_r, rsems.at[2])
        all_of(held - 1, tot, rsems.at[5])
        all_of(wins - 1, zy_r, rsems.at[4])

    @pl.when(y >= held)
    def _():
        all_of(Z * held, zy_r, rsems.at[2])
        all_of(held, tot, rsems.at[5])

    all_of(n - 1, back, qsems.at[1])
    all_of(n - 1, bbuf, qsems.at[0])
    act_copy.wait()


def finish(n, act_in, back, place, tot, act, pts, total):
    act[...] = act_in[...]
    total[...] = tot[...].reshape(padded_rows(n), C)[: chunk_rows(n)]
    rows = hilo(back[...].reshape(SLOTS, C))
    pick = onehot(iota((PTS, SLOTS), 1).astype(f32) == column(place[...]))
    pts[...] = fold(dot(pick, rows))


VM = pl.BlockSpec(memory_space=pltpu.VMEM)
SM = pl.BlockSpec(memory_space=pltpu.SMEM)
ANY = pl.BlockSpec(memory_space=pl.ANY)


def shape(*dims, dtype=f32):
    return jax.ShapeDtypeStruct(dims, dtype)


def per_device(n, wins, point_feats, owner_slab, block_slot, voxel_index, boundary, neighbours, weight_taps, cotangent):
    X, Z, K = PLACES[n]
    cap = SLOTS // n
    pad = padded_rows(n)
    held = holders(n, wins)
    per = pad // held
    scale = 1.0 / math.sqrt(wins * n * ROWS)
    vm = pltpu.VMEM
    dma = pltpu.SemaphoreType.DMA
    act, back, place, tot = pl.pallas_call(
        functools.partial(whole, n, wins, scale),
        out_shape=(shape(NB, 8, 8, 8, C), shape(n, cap, C), shape(1, PTS), shape(held, per, C)),
        in_specs=[VM, VM, VM, VM, SM, SM, ANY, ANY],
        out_specs=(ANY, VM, VM, VM),
        scratch_shapes=[
            vm((TAPS * C, C), f32),
            vm((NB, 8, 8, 8, C), f32),
            vm((NB, 8, 8, 8, C), f32),
            vm((n, cap + 1, C), f32),
            vm((n, cap + 1, C), f32),
            vm((n, C), f32),
            vm((8, 1, C), f32),
            vm((SLOTS, 2 * C), bf16),
            vm((5, 8, 8, 8, C), f32),
            vm((2, 8, 8, C), f32),
            vm((2, 8, 8, C), f32),
            vm((TAPS * C, 2 * C), bf16),
            vm((10, 10, 16, 6 * C), bf16),
            vm((ROWS, 4 * C), bf16),
            vm((4, 2 * C, 256), bf16),
            vm((TAPS * C + 8, C), f32),
            vm((3, 10, 10, 16, C), f32),
            vm((NB, 8, 8, 8, C), f32),
            vm((2, 8, 8, C), f32),
            vm((2, 8, 8, C), f32),
            vm((n, cap, C), f32),
            vm((K, X, Z, pad, C), f32),
            vm((X, Z, pad, C), f32),
            vm((X, Z, pad, C), f32),
            vm((X - 1, Z, pad, C), f32),
            vm((Z, held, per, C), f32),
            vm((Z * wins, per, C), f32),
            dma((3,)),
            dma((2,)),
            dma((4,)),
            dma((4,)),
            dma((2,)),
            dma((4,)),
            dma((6,)),
        ],
        compiler_params=pltpu.CompilerParams(vmem_limit_bytes=LIMIT, collective_id=0, has_side_effects=True),
        name="whole",
    )(
        point_feats[0],
        owner_slab.reshape(1, PTS),
        block_slot,
        voxel_index,
        boundary.reshape(2),
        neighbours[0],
        weight_taps.reshape(TAPS * C, C),
        cotangent.reshape(NB, 8, 8, 8, C),
    )
    act, pts, total = pl.pallas_call(
        functools.partial(finish, n),
        out_shape=(shape(ROWS, C), shape(PTS, C), shape(chunk_rows(n), C)),
        in_specs=[VM] * 4,
        out_specs=(VM,) * 3,
        compiler_params=pltpu.CompilerParams(vmem_limit_bytes=LIMIT),
        name="finish",
    )(act.reshape(ROWS, C), back, place, tot)
    return act[None], pts[None], total


def solution(mesh):
    n, wins = mesh.shape["slab"], mesh.shape["dp"]
    return jax.shard_map(
        functools.partial(per_device, n, wins),
        mesh=mesh,
        in_specs=(
            P("dp", "slab", None),
            P("dp", "slab", None),
            P("dp", "slab"),
            P("dp", "slab"),
            P("dp", "slab", None, None),
            P("dp", "slab", None),
            P(),
            P("dp", "slab", None),
        ),
        out_specs=(P("dp", "slab", None), P("dp", "slab", None), P("slab", None)),
        check_vma=False,
    )
```

```python
import functools
import math

import jax
import jax.numpy as jnp
from jax import lax
from jax.experimental import pallas as pl
from jax.experimental.pallas import tpu as pltpu
from jax.sharding import PartitionSpec as P

C = 128
E = 8
NB = 2
PTS = 512
VOX = 512
ROWS = NB * VOX
TAPS = 27
SLOTS = 2 * PTS
f32 = jnp.float32
bf16 = jnp.bfloat16
i32 = jnp.int32
MESH = pl.DeviceIdType.MESH
highest = lax.Precision.HIGHEST
LIMIT = 60 * 1024 * 1024
PLACES = {64: (4, 8, 2), 8: (2, 2, 2), 4: (2, 1, 2)}


def iota(shape, dim):
    return lax.broadcasted_iota(i32, shape, dim)


def split(v):
    hi = v.astype(bf16)
    return hi, (v - hi.astype(f32)).astype(bf16)


def hilo(v):
    return jnp.concatenate(split(v), axis=-1)


def onehot(where):
    return jnp.where(where, 1.0, 0.0).astype(bf16)


def fold(v):
    return v[:, :C] + v[:, C:]


def dot(a, b):
    return lax.dot_general(a, b, (((1,), (0,)), ((), ())), preferred_element_type=f32)


def column(row):
    return jnp.transpose(jnp.broadcast_to(row, (8, row.shape[1])))[:, 0:1]


def pack_points(n, me, feats, own, slot, vox, sbuf, place, idrows):
    cap = SLOTS // n
    group = C // cap
    ownr = own[...].astype(f32)
    ownc = column(ownr)
    first = iota((PTS, PTS), 0) < iota((PTS, PTS), 1)
    same = (ownc == ownr) & first
    rank = jnp.sum(jnp.where(same, 1.0, 0.0), axis=0, keepdims=True)
    placed = ownr * cap + rank
    place[...] = placed
    x2 = hilo(feats[...])
    pick = onehot(iota((SLOTS, PTS), 0).astype(f32) == placed)
    rows = fold(dot(pick, x2))
    sbuf[:, 0:cap, :] = rows.reshape(n, cap, C)
    lane = iota((PTS, C), 1).astype(f32)
    shift = (lax.rem(me, group) * cap).astype(f32)
    to_lane = jnp.where(lane == column(rank) + shift, 1.0, 0.0)
    ids = (slot[...] * VOX + vox[...]).astype(f32) + 1.0
    to_dest = jnp.where(iota((n, PTS), 0).astype(f32) == ownr, ids, 0.0)
    idrows[...] = lax.dot_general(
        to_dest, to_lane, (((1,), (0,)), ((), ())), precision=highest, preferred_element_type=f32
    )

    def put(d, carry):
        sbuf[d, cap : cap + 1, :] = idrows[pl.ds(d, 1), :]
        return carry

    lax.fori_loop(0, n, put, 0)


def prepare_taps(w, wp):
    def step(t, carry):
        rows = pl.ds(pl.multiple_of(t * 384, 384), 384)
        wp[rows, :] = hilo(w[rows, :])
        return carry

    lax.fori_loop(0, 9, step, 0)


def voxelize(n, rbuf, ids8, x2s, vis):
    cap = SLOTS // n
    group = C // cap
    x2s[...] = hilo(rbuf[:, 0:cap, :].reshape(SLOTS, C))
    ids = rbuf[:, cap : cap + 1, :].reshape(8, group, 1, C).sum(axis=1)
    ids8[...] = ids - 1.0

    def step(t, carry):
        vox = (iota((256, C), 0) + t * 256).astype(f32)
        pick = jnp.concatenate([onehot(vox == ids8[r]) for r in range(8)], axis=1)
        vis[t // 2, pl.ds(lax.rem(t, 2) * 4, 4)] = fold(dot(pick, x2s[...])).reshape(4, 8, 8, C)
        return carry

    lax.fori_loop(0, 4, step, 0)


SEC_P = ((slice(0, 1), slice(7, 8)), (slice(1, 9), slice(0, 8)), (slice(9, 10), slice(0, 1)))


def sections(which=(0, 1, 2)):
    for i in which:
        for j in range(3):
            if i == 1 and j == 1:
                for p in range(8):
                    yield i, j, slice(p + 1, p + 2), slice(1, 9), slice(p, p + 1), slice(0, 8)
            else:
                (ps, xs), (qs, ys) = SEC_P[i], SEC_P[j]
                yield i, j, ps, qs, xs, ys


def build_windows(nb, vis, S, which):
    for i, j, ps, qs, xs, ys in sections(which):
        e = 9 * i + 3 * j
        parts = ([], [], [])
        for b in range(NB):
            mid = vis[nb[b, e + 1], xs, ys]
            low = vis[nb[b, e], xs, ys]
            high = vis[nb[b, e + 2], xs, ys]
            z = iota(mid.shape, 2)
            parts[0].append(jnp.roll(jnp.where(z == 7, low, mid), 1, axis=2))
            parts[1].append(mid)
            parts[2].append(jnp.roll(jnp.where(z == 0, high, mid), -1, axis=2))
        for k in range(3):
            hi, lo = split(jnp.concatenate(parts[k], axis=2))
            S[ps, qs, :, k * C : (k + 1) * C] = hi
            S[ps, qs, :, (3 + k) * C : (4 + k) * C] = lo


def forward(S, wp, cot, act, G4, GT):
    def step(m, carry):
        total = None
        for part in range(2):
            wins = []
            for i in range(3):
                for j in range(3):
                    win = S[pl.ds(2 * m + i, 2), j : j + 8, :, part * 384 : part * 384 + 384]
                    wins.append(win.reshape(256, 384))
            got = dot(jnp.concatenate(wins, axis=1), wp[...])
            total = got if total is None else total + got
        pre = fold(total).reshape(2, 8, 16, C)
        gate = 1.0 / (1.0 + jnp.exp(-pre))
        xs = pl.ds(2 * m, 2)
        out = pre * gate
        for b in range(NB):
            act[b, xs] = out[:, :, 8 * b : 8 * b + 8]
        up = jnp.concatenate([cot[b, xs] for b in range(NB)], axis=2)
        g = (up * gate * (1.0 + pre * (1.0 - gate))).reshape(256, C)
        hi, lo = split(g)
        rows = pl.ds(pl.multiple_of(256 * m, 256), 256)
        G4[rows, :] = jnp.concatenate([hi, hi, lo, lo], axis=1)
        gt = jnp.transpose(g)
        thi, tlo = split(gt)
        GT[m, 0:C, :] = thi
        GT[m, C : 2 * C, :] = tlo
        return carry

    lax.fori_loop(0, 4, step, 0)


def weight_grad(S, GT, dW, scale, first, last):
    def step(ij, carry):
        i, j = ij // 3, lax.rem(ij, 3)
        total = None
        for m in range(4):
            win = S[pl.ds(i + 2 * m, 2), pl.ds(j, 8)].reshape(256, 768)
            got = dot(GT[m], win)
            total = got if total is None else total + got
        both = total[:C] + total[C:]
        for k in range(3):
            one = both[:, k * C : (k + 1) * C] + both[:, (3 + k) * C : (4 + k) * C]
            rows = pl.ds(pl.multiple_of(ij * 384 + k * C, C), C)
            dW[rows, :] = jnp.transpose(one) * scale
        return carry

    lax.fori_loop(first, last, step, 0)


def input_grad(G4, wp, A, first, last):
    if first == 0:
        A[...] = jnp.zeros_like(A)

    def some(ij, count):
        size = 384 * count
        w = wp[pl.ds(pl.multiple_of(ij * 384, 384), size), :]
        w2 = jnp.concatenate([w, w], axis=1)
        for m in range(4):
            y = lax.dot_general(
                G4[m * 256 : (m + 1) * 256, :], w2, (((1,), (1,)), ((), ())), preferred_element_type=f32
            )
            for c in range(count):
                i, j = (ij + c) // 3, lax.rem(ij + c, 3)
                for k in range(3):
                    col = (3 * c + k) * C
                    A[k, pl.ds(i + 2 * m, 2), pl.ds(j, 8)] += y[:, col : col + C].reshape(2, 8, 16, C)

    def step(p, carry):
        some(first + 2 * p, 2)
        return carry

    lax.fori_loop(0, (last - first) // 2, step, 0)
    if (last - first) % 2:
        some(last - 1, 1)


def carry_back(nb, A, grad, lent):
    grad[...] = jnp.zeros_like(grad)
    lent[...] = jnp.zeros_like(lent)
    for i, j, ps, qs, xs, ys in sections():
        e = 9 * i + 3 * j
        for b in range(NB):
            a0, a1, a2 = (A[k, ps, qs, 8 * b : 8 * b + 8, :] for k in range(3))
            z = iota(a0.shape, 2)
            a0 = jnp.roll(a0, -1, axis=2)
            a2 = jnp.roll(a2, 1, axis=2)
            mid = a1 + jnp.where(z == 7, 0.0, a0) + jnp.where(z == 0, 0.0, a2)
            low = jnp.where(z == 7, a0, 0.0)
            high = jnp.where(z == 0, a2, 0.0)

            def share(t):
                part = jnp.where(nb[b, e] == t, low, 0.0) + jnp.where(nb[b, e + 2] == t, high, 0.0)
                if i == 1 and j == 1:
                    return part + mid if t == b else part
                return part + jnp.where(nb[b, e + 1] == t, mid, 0.0)

            for t in range(NB):
                grad[t, xs, ys] += share(t)
            if i == 0:
                lent[0, ys] += share(2)[0]
            if i == 2:
                lent[1, ys] += share(3)[0]


def chunk_rows(n):
    return TAPS * C // n


def padded_rows(n):
    return -(-chunk_rows(n) // 8) * 8


def cut_chunks(n, dW, dwc, first, last):
    X, Z, K = PLACES[n]
    size, pad = chunk_rows(n), padded_rows(n)
    for d in range(first, last):
        rows = dW[size * d : size * d + pad, :]
        dwc[d % K, d // K // Z, d // K % Z] = rows.reshape(dwc.shape[3:])


def holders(n, wins):
    tiles = padded_rows(n) // 8
    return max(h for h in range(1, wins + 1) if tiles % h == 0)


def x_first(n, wins):
    return -(-holders(n, wins) * 4 // 7)


def greet(n, wins, me, y):
    X, Z, K = PLACES[n]
    core, z, x = lax.rem(me, K), lax.rem(me // K, Z), me // (K * Z)
    barrier = pltpu.get_barrier_semaphore()

    def hello(o, carry):
        pl.semaphore_signal(barrier, inc=1, device_id=(lax.rem(me + o, n), y), device_id_type=MESH)
        return carry

    lax.fori_loop(1, n, hello, 0)

    def hello_y(o, carry):
        to = (x * Z + lax.rem(o, Z)) * K + core
        pl.semaphore_signal(barrier, inc=1, device_id=(to, lax.rem(y + 1 + o // Z, wins)), device_id_type=MESH)
        return carry

    lax.fori_loop(0, Z * (wins - 1), hello_y, 0)

    def hello_x(o, carry):
        to = (lax.rem(x + 1 + lax.rem(o, X - 1), X) * Z + z) * K + core
        pl.semaphore_signal(barrier, inc=1, device_id=(to, lax.rem(y + 1 + o // (X - 1), wins)), device_id_type=MESH)
        return carry

    lax.fori_loop(0, (X - 1) * (wins - 1), hello_x, 0)


def greeted(n, wins):
    X, Z, K = PLACES[n]
    pl.semaphore_wait(pltpu.get_barrier_semaphore(), n - 1 + (X - 1 + Z) * (wins - 1))


def spread(n, me, y, src, dst, ssem, rsem):
    def send(o, carry):
        d = lax.rem(me + o, n)
        pltpu.make_async_remote_copy(
            src_ref=src.at[d], dst_ref=dst.at[me], send_sem=ssem, recv_sem=rsem, device_id=(d, y), device_id_type=MESH
        ).start()
        return carry

    lax.fori_loop(1, n, send, 0)


def all_of(count, ref, sem):
    pltpu.make_async_copy(ref.at[pl.ds(0, count)], ref.at[pl.ds(0, count)], sem).wait()

def both_ways(n, me, y, src, dst, sems, turn):
    copies = []
    for side in range(2):
        step = 1 if (side == 0) != turn else n - 1
        copy = pltpu.make_async_remote_copy(
            src_ref=src.at[side],
            dst_ref=dst.at[side],
            send_sem=sems.at[side],
            recv_sem=sems.at[2 + side],
            device_id=(lax.rem(me + step, n), y),
            device_id_type=MESH,
        )
        copy.start()
        copies.append(copy)
    return copies


def whole(
    n, wins, scale,
    feats, own, slot, vox, bnd, nb, w_in, cot_in,
    act, back, place, tot,
    w, cot, sbuf, rbuf, idrows, ids8, x2s, vis, hs, hr, wp, S, G4, GT, dW, A, grad, lent, lent_r, bbuf,
    dwc, core_r, xs_, x_r, zs_, zy_r, f_r, xs2, xy_r, lsems, psems, hsems, bsems, qsems, csems, rsems,
):
    X, Z, K = PLACES[n]
    cap = SLOTS // n
    held = holders(n, wins)
    front = x_first(n, wins)
    rear = held - front
    me, y = lax.axis_index("slab"), lax.axis_index("dp")
    core = lax.rem(me, K)
    z = lax.rem(me // K, Z)
    x = me // (K * Z)

    def remote(src, dst, ssem, rsem, slab, win):
        return pltpu.make_async_remote_copy(
            src_ref=src, dst_ref=dst, send_sem=ssem, recv_sem=rsem, device_id=(slab, win), device_id_type=MESH
        )

    w_copy = pltpu.make_async_copy(w_in, w, lsems.at[0])
    cot_copy = pltpu.make_async_copy(cot_in, cot, lsems.at[1])
    w_copy.start()
    cot_copy.start()
    greet(n, wins, me, y)
    pack_points(n, me, feats, own, slot, vox, sbuf, place, idrows)
    greeted(n, wins)
    spread(n, me, y, sbuf, rbuf, psems.at[0], psems.at[1])
    rbuf[me] = sbuf[me]
    vis[4] = jnp.zeros((8, 8, 8, C), f32)
    w_copy.wait()
    cot_copy.wait()
    prepare_taps(w, wp)
    all_of(n - 1, rbuf, psems.at[1])
    voxelize(n, rbuf, ids8, x2s, vis)
    hs[0] = jnp.where(bnd[1] == 1, vis[1, 7], vis[0, 7])
    hs[1] = jnp.where(bnd[0] == 1, vis[1, 0], vis[0, 0])
    copies = both_ways(n, me, y, hs, hr, hsems, False)
    build_windows(nb, vis, S, (1,))
    all_of(n - 1, sbuf, psems.at[0])
    for copy in copies:
        copy.wait()
    vis[2, 7] = hr[0]
    vis[3, 0] = hr[1]
    build_windows(nb, vis, S, (0, 2))
    forward(S, wp, cot, act, G4, GT)

    wide = X // 2

    def half_of(h):
        return pl.ds(h * wide, wide)

    def core_start(h):
        cut_chunks(n, dW, dwc, h * n // 2, (h + 1) * n // 2)
        copy = remote(
            dwc.at[1 - core, half_of(h)], core_r.at[half_of(h)], csems.at[h], csems.at[2 + h], me + 1 - 2 * core, y
        )
        copy.start()
        return copy

    def core_add(h):
        def add_core(i, carry):
            xs_[i] = dwc[core, i] + core_r[i]
            return carry

        lax.fori_loop(h * wide, (h + 1) * wide, add_core, 0)

    def x_start(h):
        def send(o, carry):
            d = lax.rem(x + o, X)

            @pl.when(d // wide == h)
            def _():
                remote(
                    xs_.at[d, :, pl.ds(0, front)], x_r.at[o - 1], rsems.at[0], rsems.at[1], (d * Z + z) * K + core, y
                ).start()

            return carry

        lax.fori_loop(1, X, send, 0)

        def send_z(o, carry):
            d = lax.rem(z + o, Z)
            remote(
                xs_.at[half_of(h), d, pl.ds(front, rear)], f_r.at[o - 1, half_of(h)], rsems.at[6], rsems.at[7],
                (x * Z + d) * K + core, y,
            ).start()
            return carry

        lax.fori_loop(1, Z, send_z, 0)

    weight_grad(S, GT, dW, scale, 0, 5)
    core_0 = core_start(0)
    weight_grad(S, GT, dW, scale, 5, 9)
    core_0.wait()
    core_add(0)
    x_start(0)
    core_1 = core_start(1)
    input_grad(G4, wp, A, 0, 4)
    core_1.wait()
    core_add(1)
    x_start(1)
    input_grad(G4, wp, A, 4, 9)
    carry_back(nb, A, grad, lent)
    copies = both_ways(n, me, y, lent, lent_r, bsems, True)
    x2s[...] = hilo(grad[...].reshape(ROWS, C))
    per = C // cap

    def pick_rows(r, carry):
        pick = onehot(iota((C, ROWS), 1).astype(f32) == column(ids8[r]))
        bbuf[pl.ds(r * per, per)] = fold(dot(pick, x2s[...])).reshape(per, cap, C)
        return carry

    lax.fori_loop(0, 8, pick_rows, 0)
    all_of(Z - 1, f_r, rsems.at[7])
    all_of(Z - 1, f_r, rsems.at[6])
    all_of(X - 1, x_r, rsems.at[1])
    all_of(X - 1, x_r, rsems.at[0])

    def add_x(i, carry):
        part = xs_[x, i, 0:front]
        for o in range(X - 1):
            part = part + x_r[o, i]
        zs_[i] = part
        return carry

    lax.fori_loop(0, Z, add_x, 0)

    def add_z(i, carry):
        part = xs_[i, z, front:held]
        for o in range(Z - 1):
            part = part + f_r[o, i]
        xs2[i] = part
        return carry

    lax.fori_loop(0, X, add_z, 0)

    def send_zy(o, carry):
        zd, yd = lax.rem(z + o // front, Z), lax.rem(o, front)

        @pl.when((o >= front) | (yd != y))
        def _():
            remote(
                zs_.at[zd, yd], zy_r.at[z * wins + y], rsems.at[2], rsems.at[3], (x * Z + zd) * K + core, yd
            ).start()

        return carry

    lax.fori_loop(0, Z * front, send_zy, 0)

    def send_xy(o, carry):
        xd, j = lax.rem(x + o // rear, X), lax.rem(o, rear)

        @pl.when((o >= rear) | (front + j != y))
        def _():
            remote(
                xs2.at[xd, j], xy_r.at[x * wins + y], rsems.at[8], rsems.at[9], (xd * Z + z) * K + core, front + j
            ).start()

        return carry

    lax.fori_loop(0, X * rear, send_xy, 0)
    for copy in copies:
        copy.wait()
    planes = []
    for t in range(NB):
        planes.append(jnp.where(bnd[0] == t, lent_r[1], 0.0).reshape(64, C))
        planes.append(jnp.where(bnd[1] == t, lent_r[0], 0.0).reshape(64, C))
    x2s[0:256] = hilo(jnp.concatenate(planes, axis=0))

    def add_planes(o, carry):
        r = lax.rem(o + me // per, 8)
        lane = iota((C, 256), 1)
        at = lane % 64 + (lane // 64 % 2) * 448 + lane // 128 * VOX
        pick = onehot(at.astype(f32) == column(ids8[r]))
        bbuf[pl.ds(r * per, per)] += fold(dot(pick, x2s[0:256])).reshape(per, cap, C)

        def send(k, carry):
            d = r * per + k

            @pl.when(d != me)
            def _():
                remote(bbuf.at[d], back.at[me], qsems.at[0], qsems.at[1], d, y).start()

            return carry

        return lax.fori_loop(0, per, send, carry)

    lax.fori_loop(0, 8, add_planes, 0)
    back[me] = bbuf[me]
    def send_y(o, carry):
        remote(tot.at[y], tot.at[y], rsems.at[4], rsems.at[5], me, lax.rem(y + o, wins)).start()
        return carry

    in_front = y < front
    in_rear = (y >= front) & (y < held)

    @pl.when(in_front)
    def _():
        all_of(Z * wins - 1, zy_r, rsems.at[3])
        zy_r[z * wins + y] = zs_[z, y]

        def add_piece(o, part):
            return part + zy_r[o]

        tot[y] = lax.fori_loop(1, Z * wins, add_piece, zy_r[0])
        lax.fori_loop(1, wins, send_y, 0)

    @pl.when(in_rear)
    def _():
        all_of(X * wins - 1, xy_r, rsems.at[9])
        xy_r[x * wins + y] = xs2[x, y - front]

        def add_piece(o, part):
            return part + xy_r[o]

        tot[y] = lax.fori_loop(1, X * wins, add_piece, xy_r[0])
        lax.fori_loop(1, wins, send_y, 0)

    @pl.when(in_front)
    def _():
        all_of(Z * front - 1, zy_r, rsems.at[2])

    @pl.when(y >= front)
    def _():
        all_of(Z * front, zy_r, rsems.at[2])

    @pl.when(in_rear)
    def _():
        all_of(X * rear - 1, xy_r, rsems.at[8])

    @pl.when((y < front) | (y >= held))
    def _():
        all_of(X * rear, xy_r, rsems.at[8])

    @pl.when(y < held)
    def _():
        all_of(held - 1, tot, rsems.at[5])
        all_of(wins - 1, zy_r, rsems.at[4])

    @pl.when(y >= held)
    def _():
        all_of(held, tot, rsems.at[5])

    all_of(n - 1, back, qsems.at[1])
    all_of(n - 1, bbuf, qsems.at[0])


def finish(n, act_in, back, place, tot, act, pts, total):
    act[...] = act_in[...]
    total[...] = tot[...].reshape(padded_rows(n), C)[: chunk_rows(n)]
    rows = hilo(back[...].reshape(SLOTS, C))
    pick = onehot(iota((PTS, SLOTS), 1).astype(f32) == column(place[...]))
    pts[...] = fold(dot(pick, rows))


VM = pl.BlockSpec(memory_space=pltpu.VMEM)
SM = pl.BlockSpec(memory_space=pltpu.SMEM)
ANY = pl.BlockSpec(memory_space=pl.ANY)


def shape(*dims, dtype=f32):
    return jax.ShapeDtypeStruct(dims, dtype)


def per_device(n, wins, point_feats, owner_slab, block_slot, voxel_index, boundary, neighbours, weight_taps, cotangent):
    X, Z, K = PLACES[n]
    cap = SLOTS // n
    pad = padded_rows(n)
    held = holders(n, wins)
    per = pad // held
    front = x_first(n, wins)
    rear = held - front
    scale = 1.0 / math.sqrt(wins * n * ROWS)
    vm = pltpu.VMEM
    dma = pltpu.SemaphoreType.DMA
    act, back, place, tot = pl.pallas_call(
        functools.partial(whole, n, wins, scale),
        out_shape=(vm((NB, 8, 8, 8, C), f32), vm((n, cap, C), f32), vm((1, PTS), f32), vm((held, per, C), f32)),
        in_specs=[VM, VM, VM, VM, SM, SM, ANY, ANY],
        out_specs=(VM,) * 4,
        scratch_shapes=[
            vm((TAPS * C, C), f32),
            vm((NB, 8, 8, 8, C), f32),
            vm((n, cap + 1, C), f32),
            vm((n, cap + 1, C), f32),
            vm((n, C), f32),
            vm((8, 1, C), f32),
            vm((SLOTS, 2 * C), bf16),
            vm((5, 8, 8, 8, C), f32),
            vm((2, 8, 8, C), f32),
            vm((2, 8, 8, C), f32),
            vm((TAPS * C, 2 * C), bf16),
            vm((10, 10, 16, 6 * C), bf16),
            vm((ROWS, 4 * C), bf16),
            vm((4, 2 * C, 256), bf16),
            vm((TAPS * C + 8, C), f32),
            vm((3, 10, 10, 16, C), f32),
            vm((NB, 8, 8, 8, C), f32),
            vm((2, 8, 8, C), f32),
            vm((2, 8, 8, C), f32),
            vm((n, cap, C), f32),
            vm((K, X, Z, held, per, C), f32),
            vm((X, Z, held, per, C), f32),
            vm((X, Z, held, per, C), f32),
            vm((X - 1, Z, front, per, C), f32),
            vm((Z, front, per, C), f32),
            vm((Z * wins, per, C), f32),
            vm((Z - 1, X, rear, per, C), f32),
            vm((X, rear, per, C), f32),
            vm((X * wins, per, C), f32),
            dma((2,)),
            dma((2,)),
            dma((4,)),
            dma((4,)),
            dma((2,)),
            dma((4,)),
            dma((10,)),
        ],
        compiler_params=pltpu.CompilerParams(vmem_limit_bytes=LIMIT, collective_id=0, has_side_effects=True),
        name="whole",
    )(
        point_feats[0],
        owner_slab.reshape(1, PTS),
        block_slot,
        voxel_index,
        boundary.reshape(2),
        neighbours[0],
        weight_taps.reshape(TAPS * C, C),
        cotangent.reshape(NB, 8, 8, 8, C),
    )
    act, pts, total = pl.pallas_call(
        functools.partial(finish, n),
        out_shape=(shape(ROWS, C), shape(PTS, C), shape(chunk_rows(n), C)),
        in_specs=[VM] * 4,
        out_specs=(VM,) * 3,
        compiler_params=pltpu.CompilerParams(vmem_limit_bytes=LIMIT // 3),
        name="finish",
    )(act.reshape(ROWS, C), back, place, tot)
    return act[None], pts[None], total


def solution(mesh):
    n, wins = mesh.shape["slab"], mesh.shape["dp"]
    return jax.shard_map(
        functools.partial(per_device, n, wins),
        mesh=mesh,
        in_specs=(
            P("dp", "slab", None),
            P("dp", "slab", None),
            P("dp", "slab"),
            P("dp", "slab"),
            P("dp", "slab", None, None),
            P("dp", "slab", None),
            P(),
            P("dp", "slab", None),
        ),
        out_specs=(P("dp", "slab", None), P("dp", "slab", None), P("slab", None)),
        check_vma=False,
    )
```

```python
import functools
import math

import jax
import jax.numpy as jnp
from jax import lax
from jax.experimental import pallas as pl
from jax.experimental.pallas import tpu as pltpu
from jax.sharding import PartitionSpec as P

C = 128
E = 8
NB = 2
PTS = 512
VOX = 512
ROWS = NB * VOX
TAPS = 27
SLOTS = 2 * PTS
f32 = jnp.float32
bf16 = jnp.bfloat16
i32 = jnp.int32
MESH = pl.DeviceIdType.MESH
highest = lax.Precision.HIGHEST
LIMIT = 60 * 1024 * 1024
PLACES = {64: (4, 8, 2), 8: (2, 2, 2), 4: (2, 1, 2)}


def iota(shape, dim):
    return lax.broadcasted_iota(i32, shape, dim)


def split(v):
    hi = v.astype(bf16)
    return hi, (v - hi.astype(f32)).astype(bf16)


def hilo(v):
    return jnp.concatenate(split(v), axis=-1)


def onehot(where):
    return jnp.where(where, 1.0, 0.0).astype(bf16)


def fold(v):
    return v[:, :C] + v[:, C:]


def dot(a, b):
    return lax.dot_general(a, b, (((1,), (0,)), ((), ())), preferred_element_type=f32)


def column(row):
    return jnp.transpose(jnp.broadcast_to(row, (8, row.shape[1])))[:, 0:1]


def pack_points(n, me, feats, arrived, own, slot, vox, sbuf, place, idrows):
    cap = SLOTS // n
    group = C // cap
    ownr = own[...].astype(f32)
    ownc = column(ownr)
    first = iota((PTS, PTS), 0) < iota((PTS, PTS), 1)
    same = (ownc == ownr) & first
    rank = jnp.sum(jnp.where(same, 1.0, 0.0), axis=0, keepdims=True)
    placed = ownr * cap + rank
    place[...] = placed
    pick = onehot(iota((SLOTS, PTS), 0).astype(f32) == placed)
    arrived()
    x2 = hilo(feats[...])
    rows = fold(dot(pick, x2))
    sbuf[:, 0:cap, :] = rows.reshape(n, cap, C)
    lane = iota((PTS, C), 1).astype(f32)
    shift = (lax.rem(me, group) * cap).astype(f32)
    to_lane = jnp.where(lane == column(rank) + shift, 1.0, 0.0)
    ids = (slot[...] * VOX + vox[...]).astype(f32) + 1.0
    to_dest = jnp.where(iota((n, PTS), 0).astype(f32) == ownr, ids, 0.0)
    idrows[...] = lax.dot_general(
        to_dest, to_lane, (((1,), (0,)), ((), ())), precision=highest, preferred_element_type=f32
    )

    def put(d, carry):
        sbuf[d, cap : cap + 1, :] = idrows[pl.ds(d, 1), :]
        return carry

    lax.fori_loop(0, n, put, 0)


def prepare_taps(w, wp):
    def step(t, carry):
        rows = pl.ds(pl.multiple_of(t * 384, 384), 384)
        wp[rows, :] = hilo(w[rows, :])
        return carry

    lax.fori_loop(0, 9, step, 0)


def voxelize(n, rbuf, ids8, x2s, vis):
    cap = SLOTS // n
    group = C // cap
    x2s[...] = hilo(rbuf[:, 0:cap, :].reshape(SLOTS, C))
    ids = rbuf[:, cap : cap + 1, :].reshape(8, group, 1, C).sum(axis=1)
    ids8[...] = ids - 1.0

    def step(t, carry):
        vox = (iota((256, C), 0) + t * 256).astype(f32)
        pick = jnp.concatenate([onehot(vox == ids8[r]) for r in range(8)], axis=1)
        vis[t // 2, pl.ds(lax.rem(t, 2) * 4, 4)] = fold(dot(pick, x2s[...])).reshape(4, 8, 8, C)
        return carry

    lax.fori_loop(0, 4, step, 0)


SEC_P = ((slice(0, 1), slice(7, 8)), (slice(1, 9), slice(0, 8)), (slice(9, 10), slice(0, 1)))


def sections(which=(0, 1, 2)):
    for i in which:
        for j in range(3):
            if i == 1 and j == 1:
                for p in range(8):
                    yield i, j, slice(p + 1, p + 2), slice(1, 9), slice(p, p + 1), slice(0, 8)
            else:
                (ps, xs), (qs, ys) = SEC_P[i], SEC_P[j]
                yield i, j, ps, qs, xs, ys


def build_windows(nb, vis, S, which):
    for i, j, ps, qs, xs, ys in sections(which):
        e = 9 * i + 3 * j
        parts = ([], [], [])
        for b in range(NB):
            mid = vis[nb[b, e + 1], xs, ys]
            low = vis[nb[b, e], xs, ys]
            high = vis[nb[b, e + 2], xs, ys]
            z = iota(mid.shape, 2)
            parts[0].append(jnp.roll(jnp.where(z == 7, low, mid), 1, axis=2))
            parts[1].append(mid)
            parts[2].append(jnp.roll(jnp.where(z == 0, high, mid), -1, axis=2))
        for k in range(3):
            hi, lo = split(jnp.concatenate(parts[k], axis=2))
            S[ps, qs, :, k * C : (k + 1) * C] = hi
            S[ps, qs, :, (3 + k) * C : (4 + k) * C] = lo


def forward(S, wp, cot, act, G4, GT):
    def step(m, carry):
        total = None
        for part in range(2):
            wins = []
            for i in range(3):
                for j in range(3):
                    win = S[pl.ds(2 * m + i, 2), j : j + 8, :, part * 384 : part * 384 + 384]
                    wins.append(win.reshape(256, 384))
            got = dot(jnp.concatenate(wins, axis=1), wp[...])
            total = got if total is None else total + got
        pre = fold(total).reshape(2, 8, 16, C)
        gate = 1.0 / (1.0 + jnp.exp(-pre))
        xs = pl.ds(2 * m, 2)
        out = pre * gate
        for b in range(NB):
            act[b, xs] = out[:, :, 8 * b : 8 * b + 8]
        up = jnp.concatenate([cot[b, xs] for b in range(NB)], axis=2)
        g = (up * gate * (1.0 + pre * (1.0 - gate))).reshape(256, C)
        hi, lo = split(g)
        rows = pl.ds(pl.multiple_of(256 * m, 256), 256)
        G4[rows, :] = jnp.concatenate([hi, hi, lo, lo], axis=1)
        gt = jnp.transpose(g)
        thi, tlo = split(gt)
        GT[m, 0:C, :] = thi
        GT[m, C : 2 * C, :] = tlo
        return carry

    lax.fori_loop(0, 4, step, 0)


def weight_grad(S, GT, dW, scale, first, last):
    def step(ij, carry):
        i, j = ij // 3, lax.rem(ij, 3)
        total = None
        for m in range(4):
            win = S[pl.ds(i + 2 * m, 2), pl.ds(j, 8)].reshape(256, 768)
            got = dot(GT[m], win)
            total = got if total is None else total + got
        both = total[:C] + total[C:]
        for k in range(3):
            one = both[:, k * C : (k + 1) * C] + both[:, (3 + k) * C : (4 + k) * C]
            rows = pl.ds(pl.multiple_of(ij * 384 + k * C, C), C)
            dW[rows, :] = jnp.transpose(one) * scale
        return carry

    lax.fori_loop(first, last, step, 0)


def input_grad(G4, wp, A, first, last):
    if first == 0:
        A[...] = jnp.zeros_like(A)

    def some(ij, count):
        size = 384 * count
        w = wp[pl.ds(pl.multiple_of(ij * 384, 384), size), :]
        w2 = jnp.concatenate([w, w], axis=1)
        for m in range(4):
            y = lax.dot_general(
                G4[m * 256 : (m + 1) * 256, :], w2, (((1,), (1,)), ((), ())), preferred_element_type=f32
            )
            for c in range(count):
                i, j = (ij + c) // 3, lax.rem(ij + c, 3)
                for k in range(3):
                    col = (3 * c + k) * C
                    A[k, pl.ds(i + 2 * m, 2), pl.ds(j, 8)] += y[:, col : col + C].reshape(2, 8, 16, C)

    def step(p, carry):
        some(first + 2 * p, 2)
        return carry

    lax.fori_loop(0, (last - first) // 2, step, 0)
    if (last - first) % 2:
        some(last - 1, 1)


def carry_back(nb, A, grad, lent):
    grad[...] = jnp.zeros_like(grad)
    lent[...] = jnp.zeros_like(lent)
    for i, j, ps, qs, xs, ys in sections():
        e = 9 * i + 3 * j
        for b in range(NB):
            a0, a1, a2 = (A[k, ps, qs, 8 * b : 8 * b + 8, :] for k in range(3))
            z = iota(a0.shape, 2)
            a0 = jnp.roll(a0, -1, axis=2)
            a2 = jnp.roll(a2, 1, axis=2)
            mid = a1 + jnp.where(z == 7, 0.0, a0) + jnp.where(z == 0, 0.0, a2)
            low = jnp.where(z == 7, a0, 0.0)
            high = jnp.where(z == 0, a2, 0.0)

            def share(t):
                part = jnp.where(nb[b, e] == t, low, 0.0) + jnp.where(nb[b, e + 2] == t, high, 0.0)
                if i == 1 and j == 1:
                    return part + mid if t == b else part
                return part + jnp.where(nb[b, e + 1] == t, mid, 0.0)

            for t in range(NB):
                grad[t, xs, ys] += share(t)
            if i == 0:
                lent[0, ys] += share(2)[0]
            if i == 2:
                lent[1, ys] += share(3)[0]


def chunk_rows(n):
    return TAPS * C // n


def padded_rows(n):
    return -(-chunk_rows(n) // 8) * 8


def cut_chunks(n, dW, dwc, first, last):
    X, Z, K = PLACES[n]
    size, pad = chunk_rows(n), padded_rows(n)
    for d in range(first, last):
        rows = dW[size * d : size * d + pad, :]
        dwc[d % K, d // K // Z, d // K % Z] = rows.reshape(dwc.shape[3:])


def holders(n, wins):
    tiles = padded_rows(n) // 8
    return max(h for h in range(1, wins + 1) if tiles % h == 0)


def x_first(n, wins):
    return -(-holders(n, wins) * 4 // 7)


def greet(n, wins, me, y):
    X, Z, K = PLACES[n]
    core, z, x = lax.rem(me, K), lax.rem(me // K, Z), me // (K * Z)
    barrier = pltpu.get_barrier_semaphore()

    def hello(o, carry):
        pl.semaphore_signal(barrier, inc=1, device_id=(lax.rem(me + o, n), y), device_id_type=MESH)
        return carry

    lax.fori_loop(1, n, hello, 0)

    def hello_y(o, carry):
        to = (x * Z + lax.rem(o, Z)) * K + core
        pl.semaphore_signal(barrier, inc=1, device_id=(to, lax.rem(y + 1 + o // Z, wins)), device_id_type=MESH)
        return carry

    lax.fori_loop(0, Z * (wins - 1), hello_y, 0)

    def hello_x(o, carry):
        to = (lax.rem(x + 1 + lax.rem(o, X - 1), X) * Z + z) * K + core
        pl.semaphore_signal(barrier, inc=1, device_id=(to, lax.rem(y + 1 + o // (X - 1), wins)), device_id_type=MESH)
        return carry

    lax.fori_loop(0, (X - 1) * (wins - 1), hello_x, 0)


def greeted(n, wins):
    X, Z, K = PLACES[n]
    pl.semaphore_wait(pltpu.get_barrier_semaphore(), n - 1 + (X - 1 + Z) * (wins - 1))


def spread(n, me, y, src, dst, ssem, rsem):
    def send(o, carry):
        d = lax.rem(me + o, n)
        pltpu.make_async_remote_copy(
            src_ref=src.at[d], dst_ref=dst.at[me], send_sem=ssem, recv_sem=rsem, device_id=(d, y), device_id_type=MESH
        ).start()
        return carry

    lax.fori_loop(1, n, send, 0)


def all_of(count, ref, sem):
    pltpu.make_async_copy(ref.at[pl.ds(0, count)], ref.at[pl.ds(0, count)], sem).wait()

def both_ways(n, me, y, src, dst, sems, turn):
    copies = []
    for side in range(2):
        step = 1 if (side == 0) != turn else n - 1
        copy = pltpu.make_async_remote_copy(
            src_ref=src.at[side],
            dst_ref=dst.at[side],
            send_sem=sems.at[side],
            recv_sem=sems.at[2 + side],
            device_id=(lax.rem(me + step, n), y),
            device_id_type=MESH,
        )
        copy.start()
        copies.append(copy)
    return copies


def whole(
    n, wins, scale,
    feats_in, own, slot, vox, bnd, nb, w_in, cot_in,
    act, back, place, tot,
    feats, w, cot, sbuf, rbuf, idrows, ids8, x2s, vis, hs, hr, wp, S, G4, GT, dW, A, grad, lent, lent_r, bbuf,
    dwc, core_r, xs_, x_r, zs_, zy_r, f_r, xs2, xy_r, lsems, psems, hsems, bsems, qsems, csems, rsems,
):
    X, Z, K = PLACES[n]
    cap = SLOTS // n
    held = holders(n, wins)
    front = x_first(n, wins)
    rear = held - front
    me, y = lax.axis_index("slab"), lax.axis_index("dp")
    core = lax.rem(me, K)
    z = lax.rem(me // K, Z)
    x = me // (K * Z)

    def remote(src, dst, ssem, rsem, slab, win):
        return pltpu.make_async_remote_copy(
            src_ref=src, dst_ref=dst, send_sem=ssem, recv_sem=rsem, device_id=(slab, win), device_id_type=MESH
        )

    w_copy = pltpu.make_async_copy(w_in, w, lsems.at[0])
    cot_copy = pltpu.make_async_copy(cot_in, cot, lsems.at[1])
    feats_copy = pltpu.make_async_copy(feats_in, feats, lsems.at[2])
    feats_copy.start()
    greet(n, wins, me, y)
    w_copy.start()
    cot_copy.start()
    pack_points(n, me, feats, feats_copy.wait, own, slot, vox, sbuf, place, idrows)
    greeted(n, wins)
    spread(n, me, y, sbuf, rbuf, psems.at[0], psems.at[1])
    rbuf[me] = sbuf[me]
    vis[4] = jnp.zeros((8, 8, 8, C), f32)
    w_copy.wait()
    cot_copy.wait()
    prepare_taps(w, wp)
    all_of(n - 1, rbuf, psems.at[1])
    voxelize(n, rbuf, ids8, x2s, vis)
    hs[0] = jnp.where(bnd[1] == 1, vis[1, 7], vis[0, 7])
    hs[1] = jnp.where(bnd[0] == 1, vis[1, 0], vis[0, 0])
    copies = both_ways(n, me, y, hs, hr, hsems, False)
    build_windows(nb, vis, S, (1,))
    all_of(n - 1, sbuf, psems.at[0])
    for copy in copies:
        copy.wait()
    vis[2, 7] = hr[0]
    vis[3, 0] = hr[1]
    build_windows(nb, vis, S, (0, 2))
    forward(S, wp, cot, act, G4, GT)

    wide = X // 2

    def half_of(h):
        return pl.ds(h * wide, wide)

    def core_start(h):
        cut_chunks(n, dW, dwc, h * n // 2, (h + 1) * n // 2)
        copy = remote(
            dwc.at[1 - core, half_of(h)], core_r.at[half_of(h)], csems.at[h], csems.at[2 + h], me + 1 - 2 * core, y
        )
        copy.start()
        return copy

    def core_add(h):
        def add_core(i, carry):
            xs_[i] = dwc[core, i] + core_r[i]
            return carry

        lax.fori_loop(h * wide, (h + 1) * wide, add_core, 0)

    def x_start(h):
        def send(o, carry):
            d = lax.rem(x + o, X)

            @pl.when(d // wide == h)
            def _():
                remote(
                    xs_.at[d, :, pl.ds(0, front)], x_r.at[o - 1], rsems.at[0], rsems.at[1], (d * Z + z) * K + core, y
                ).start()

            return carry

        lax.fori_loop(1, X, send, 0)

        def send_z(o, carry):
            d = lax.rem(z + o, Z)
            remote(
                xs_.at[half_of(h), d, pl.ds(front, rear)], f_r.at[o - 1, half_of(h)], rsems.at[6], rsems.at[7],
                (x * Z + d) * K + core, y,
            ).start()
            return carry

        lax.fori_loop(1, Z, send_z, 0)

    weight_grad(S, GT, dW, scale, 0, 5)
    core_0 = core_start(0)
    weight_grad(S, GT, dW, scale, 5, 9)
    core_0.wait()
    core_add(0)
    x_start(0)
    core_1 = core_start(1)
    input_grad(G4, wp, A, 0, 4)
    core_1.wait()
    core_add(1)
    x_start(1)
    input_grad(G4, wp, A, 4, 9)
    carry_back(nb, A, grad, lent)
    copies = both_ways(n, me, y, lent, lent_r, bsems, True)
    x2s[...] = hilo(grad[...].reshape(ROWS, C))
    per = C // cap

    def pick_rows(r, carry):
        pick = onehot(iota((C, ROWS), 1).astype(f32) == column(ids8[r]))
        bbuf[pl.ds(r * per, per)] = fold(dot(pick, x2s[...])).reshape(per, cap, C)
        return carry

    lax.fori_loop(0, 8, pick_rows, 0)
    all_of(Z - 1, f_r, rsems.at[7])
    all_of(Z - 1, f_r, rsems.at[6])
    all_of(X - 1, x_r, rsems.at[1])
    all_of(X - 1, x_r, rsems.at[0])

    def add_x(i, carry):
        part = xs_[x, i, 0:front]
        for o in range(X - 1):
            part = part + x_r[o, i]
        zs_[i] = part
        return carry

    lax.fori_loop(0, Z, add_x, 0)

    def add_z(i, carry):
        part = xs_[i, z, front:held]
        for o in range(Z - 1):
            part = part + f_r[o, i]
        xs2[i] = part
        return carry

    lax.fori_loop(0, X, add_z, 0)

    def send_zy(o, carry):
        zd, yd = lax.rem(z + o // front, Z), lax.rem(o, front)

        @pl.when((o >= front) | (yd != y))
        def _():
            remote(
                zs_.at[zd, yd], zy_r.at[z * wins + y], rsems.at[2], rsems.at[3], (x * Z + zd) * K + core, yd
            ).start()

        return carry

    lax.fori_loop(0, Z * front, send_zy, 0)

    def send_xy(o, carry):
        xd, j = lax.rem(x + o // rear, X), lax.rem(o, rear)

        @pl.when((o >= rear) | (front + j != y))
        def _():
            remote(
                xs2.at[xd, j], xy_r.at[x * wins + y], rsems.at[8], rsems.at[9], (xd * Z + z) * K + core, front + j
            ).start()

        return carry

    lax.fori_loop(0, X * rear, send_xy, 0)
    for copy in copies:
        copy.wait()
    planes = []
    for t in range(NB):
        planes.append(jnp.where(bnd[0] == t, lent_r[1], 0.0).reshape(64, C))
        planes.append(jnp.where(bnd[1] == t, lent_r[0], 0.0).reshape(64, C))
    x2s[0:256] = hilo(jnp.concatenate(planes, axis=0))

    def add_planes(o, carry):
        r = lax.rem(o + me // per, 8)
        lane = iota((C, 256), 1)
        at = lane % 64 + (lane // 64 % 2) * 448 + lane // 128 * VOX
        pick = onehot(at.astype(f32) == column(ids8[r]))
        bbuf[pl.ds(r * per, per)] += fold(dot(pick, x2s[0:256])).reshape(per, cap, C)

        def send(k, carry):
            d = r * per + k

            @pl.when(d != me)
            def _():
                remote(bbuf.at[d], back.at[me], qsems.at[0], qsems.at[1], d, y).start()

            return carry

        return lax.fori_loop(0, per, send, carry)

    lax.fori_loop(0, 8, add_planes, 0)
    back[me] = bbuf[me]
    def send_y(o, carry):
        remote(tot.at[y], tot.at[y], rsems.at[4], rsems.at[5], me, lax.rem(y + o, wins)).start()
        return carry

    in_front = y < front
    in_rear = (y >= front) & (y < held)

    @pl.when(in_front)
    def _():
        all_of(Z * wins - 1, zy_r, rsems.at[3])
        zy_r[z * wins + y] = zs_[z, y]

        def add_piece(o, part):
            return part + zy_r[o]

        tot[y] = lax.fori_loop(1, Z * wins, add_piece, zy_r[0])
        lax.fori_loop(1, wins, send_y, 0)

    @pl.when(in_rear)
    def _():
        all_of(X * wins - 1, xy_r, rsems.at[9])
        xy_r[x * wins + y] = xs2[x, y - front]

        def add_piece(o, part):
            return part + xy_r[o]

        tot[y] = lax.fori_loop(1, X * wins, add_piece, xy_r[0])
        lax.fori_loop(1, wins, send_y, 0)

    @pl.when(in_front)
    def _():
        all_of(Z * front - 1, zy_r, rsems.at[2])

    @pl.when(y >= front)
    def _():
        all_of(Z * front, zy_r, rsems.at[2])

    @pl.when(in_rear)
    def _():
        all_of(X * rear - 1, xy_r, rsems.at[8])

    @pl.when((y < front) | (y >= held))
    def _():
        all_of(X * rear, xy_r, rsems.at[8])

    @pl.when(y < held)
    def _():
        all_of(held - 1, tot, rsems.at[5])
        all_of(wins - 1, zy_r, rsems.at[4])

    @pl.when(y >= held)
    def _():
        all_of(held, tot, rsems.at[5])

    all_of(n - 1, back, qsems.at[1])
    all_of(n - 1, bbuf, qsems.at[0])


def finish(n, act_in, back, place, tot, act, pts, total):
    act[...] = act_in[...]
    total[...] = tot[...].reshape(padded_rows(n), C)[: chunk_rows(n)]
    rows = hilo(back[...].reshape(SLOTS, C))
    pick = onehot(iota((PTS, SLOTS), 1).astype(f32) == column(place[...]))
    pts[...] = fold(dot(pick, rows))


VM = pl.BlockSpec(memory_space=pltpu.VMEM)
SM = pl.BlockSpec(memory_space=pltpu.SMEM)
ANY = pl.BlockSpec(memory_space=pl.ANY)


def shape(*dims, dtype=f32):
    return jax.ShapeDtypeStruct(dims, dtype)


def per_device(n, wins, point_feats, owner_slab, block_slot, voxel_index, boundary, neighbours, weight_taps, cotangent):
    X, Z, K = PLACES[n]
    cap = SLOTS // n
    pad = padded_rows(n)
    held = holders(n, wins)
    per = pad // held
    front = x_first(n, wins)
    rear = held - front
    scale = 1.0 / math.sqrt(wins * n * ROWS)
    vm = pltpu.VMEM
    dma = pltpu.SemaphoreType.DMA
    act, back, place, tot = pl.pallas_call(
        functools.partial(whole, n, wins, scale),
        out_shape=(vm((NB, 8, 8, 8, C), f32), vm((n, cap, C), f32), vm((1, PTS), f32), vm((held, per, C), f32)),
        in_specs=[ANY, VM, VM, VM, SM, SM, ANY, ANY],
        out_specs=(VM,) * 4,
        scratch_shapes=[
            vm((PTS, C), f32),
            vm((TAPS * C, C), f32),
            vm((NB, 8, 8, 8, C), f32),
            vm((n, cap + 1, C), f32),
            vm((n, cap + 1, C), f32),
            vm((n, C), f32),
            vm((8, 1, C), f32),
            vm((SLOTS, 2 * C), bf16),
            vm((5, 8, 8, 8, C), f32),
            vm((2, 8, 8, C), f32),
            vm((2, 8, 8, C), f32),
            vm((TAPS * C, 2 * C), bf16),
            vm((10, 10, 16, 6 * C), bf16),
            vm((ROWS, 4 * C), bf16),
            vm((4, 2 * C, 256), bf16),
            vm((TAPS * C + 8, C), f32),
            vm((3, 10, 10, 16, C), f32),
            vm((NB, 8, 8, 8, C), f32),
            vm((2, 8, 8, C), f32),
            vm((2, 8, 8, C), f32),
            vm((n, cap, C), f32),
            vm((K, X, Z, held, per, C), f32),
            vm((X, Z, held, per, C), f32),
            vm((X, Z, held, per, C), f32),
            vm((X - 1, Z, front, per, C), f32),
            vm((Z, front, per, C), f32),
            vm((Z * wins, per, C), f32),
            vm((Z - 1, X, rear, per, C), f32),
            vm((X, rear, per, C), f32),
            vm((X * wins, per, C), f32),
            dma((3,)),
            dma((2,)),
            dma((4,)),
            dma((4,)),
            dma((2,)),
            dma((4,)),
            dma((10,)),
        ],
        compiler_params=pltpu.CompilerParams(vmem_limit_bytes=LIMIT, collective_id=0, has_side_effects=True),
        name="whole",
    )(
        point_feats[0],
        owner_slab.reshape(1, PTS),
        block_slot,
        voxel_index,
        boundary.reshape(2),
        neighbours[0],
        weight_taps.reshape(TAPS * C, C),
        cotangent.reshape(NB, 8, 8, 8, C),
    )
    act, pts, total = pl.pallas_call(
        functools.partial(finish, n),
        out_shape=(shape(ROWS, C), shape(PTS, C), shape(chunk_rows(n), C)),
        in_specs=[VM] * 4,
        out_specs=(VM,) * 3,
        compiler_params=pltpu.CompilerParams(vmem_limit_bytes=LIMIT // 3),
        name="finish",
    )(act.reshape(ROWS, C), back, place, tot)
    return act[None], pts[None], total


def solution(mesh):
    n, wins = mesh.shape["slab"], mesh.shape["dp"]
    return jax.shard_map(
        functools.partial(per_device, n, wins),
        mesh=mesh,
        in_specs=(
            P("dp", "slab", None),
            P("dp", "slab", None),
            P("dp", "slab"),
            P("dp", "slab"),
            P("dp", "slab", None, None),
            P("dp", "slab", None),
            P(),
            P("dp", "slab", None),
        ),
        out_specs=(P("dp", "slab", None), P("dp", "slab", None), P("slab", None)),
        check_vma=False,
    )
```
